32 devices in a mesh: groups: 2 (over x), clus: 16 (over z, y, core).
Axes of the slice: x: 2, y: 2, z: 4, core: 2. Of those that a mesh axis runs over, the one named last changes fastest.
Arguments:
- mesh_current: float32 [2, 131072], P(None, ('groups', 'clus')), parts along dimension 1, may hold values from -6 to 6
- branch_entry: int32 [2, 262144], P(None, ('groups', 'clus')), parts along dimension 1, may hold values from 0 to 6143, as said below
- branch_sign: int32 [2, 262144], P(None, ('groups', 'clus')), parts along dimension 1, may hold values from 0 to 1
- need_slots: int32 [512, 128], P(('groups', 'clus')), parts along dimension 0, may hold values from -1 to 4095, as said below
- resistance: float32 [262144], P(('groups', 'clus')), parts along dimension 0, may hold values from 0.3 to 3
- near_blocks: bfloat16 [2048, 4, 128, 128], P(('groups', 'clus')), parts along dimension 0, may hold values from -0.25 to 0.25
- near_source: int32 [2048, 4], P(('groups', 'clus')), parts along dimension 0, may hold values from 0 to 63
- basis_in: bfloat16 [2048, 32, 128], P(('groups', 'clus')), parts along dimension 0, may hold values from -0.5 to 0.5
- coupling: bfloat16 [2048, 16, 32, 32], P(('groups', 'clus')), parts along dimension 0, may hold values from -0.25 to 0.25
- basis_out: bfloat16 [2048, 32, 128], P(('groups', 'clus')), parts along dimension 0, may hold values from -1 to 1
- admissible: int32 [2048, 16], P(('groups', 'clus')), parts along dimension 0, may hold values from 0 to 1023, as said below
- port_mesh: int32 [128], P('groups'), parts along dimension 0, may hold values from 0 to 65535, as said below
- port_coupling: float32 [2, 64, 64], replicated, may hold values from -0.75 to 0.75
Outputs:
- mesh_voltage: float32 [2, 131072], P(None, ('groups', 'clus')), parts along dimension 1
The draws below stay inside these ranges and needn't reach their ends.
There are 2 independent parts, one for each index of `groups`. The reference program is written for one: setup_inputs(seed, part) draws one part's arguments, and reference() takes and returns one part's arrays. A program takes and returns all parts, laid end to end along the dimension named above; an argument that names none is the same for every part. Nothing has to cross between parts.
Inputs may be any that keep to these rules, and one draw needn't show every extreme that they name: `need_slots`: row d * 16 + p holds distinct meshes of device p, counted from 0 within it, in its first slots and -1 in the rest. Row d * 16 + d is all -1; row d * 16 + (d + 1) % 16 has no -1. `branch_entry`: A value below 4096 is a mesh of the branch's own device d. Any other value is 4096 + p * 128 + s with p != d and slot s of row d * 16 + p of need_slots not -1. `admissible`: entry k of row t is (t + k * 64 + o) % 1024 with 1 <= o < 64; the entries of a row are distinct and never t. `port_mesh`: distinct meshes.
All inputs are finite; a program needn't handle non-finite values.
Results may differ from the reference program's by a relative error of at most 0.0021.
Values may be sent and summed in bfloat16 or wider, within the bound.
A program may use at most 320 MiB of HBM per device.

```python
import math
import jax
import jax.numpy as jnp
from jax import lax

TILE_SIZE = 128
FAR_RANK = 32
NEAR_COUNT = 4
FAR_COUNT = 16
ENTRIES = 2
SLOT_COUNT = 128
PORT_COUNT = 64
TILE_DEV = 64
BRANCH_DEV = 8192
MESH_DEV = 4096
TILES = 1024
BRANCHES = 131072
MESHES = 65536
N_CLUS = 16


def slot_counts(key):
    drawn_counts = jax.random.randint(jax.random.fold_in(key, 11), (N_CLUS, N_CLUS), 1, SLOT_COUNT + 1)
    device_rows = jnp.arange(N_CLUS, dtype=jnp.int32)
    filled = device_rows[None, :] == (device_rows[:, None] + 1) % N_CLUS
    counts = jnp.where(filled, SLOT_COUNT, drawn_counts)
    return jnp.where(device_rows[:, None] == device_rows[None, :], 0, counts).astype(jnp.int32)


def first_meshes(one_key):
    return jax.random.permutation(one_key, MESH_DEV)[:SLOT_COUNT].astype(jnp.int32)


def draw_need_slots(key, part):
    counts = slot_counts(key).reshape(-1)
    mesh_keys = jax.random.split(jax.random.fold_in(key, 12), N_CLUS * N_CLUS)
    chosen = jax.vmap(first_meshes)(mesh_keys)
    places = jnp.arange(SLOT_COUNT, dtype=jnp.int32)
    return jnp.where(places[None, :] < counts[:, None], chosen, -1).astype(jnp.int32)


def draw_branch_entry(key, part):
    counts = slot_counts(key)
    entry_shape = (ENTRIES, BRANCHES)
    owner_device = jnp.broadcast_to(jnp.arange(BRANCHES, dtype=jnp.int32) // BRANCH_DEV, entry_shape)
    remote = jax.random.randint(jax.random.fold_in(key, 21), entry_shape, 0, 4) == 0
    peer_step = jax.random.randint(jax.random.fold_in(key, 22), entry_shape, 1, N_CLUS)
    peer = (owner_device + peer_step) % N_CLUS
    filled = counts[owner_device, peer]
    slot_place = jax.random.randint(jax.random.fold_in(key, 23), entry_shape, 0, filled)
    local_mesh = jax.random.randint(jax.random.fold_in(key, 24), entry_shape, 0, MESH_DEV)
    forced = (jnp.arange(BRANCHES, dtype=jnp.int32)[None, :] % BRANCH_DEV == 0) & (jnp.arange(ENTRIES, dtype=jnp.int32)[:, None] == ENTRIES - 1)
    peer = jnp.where(forced, (owner_device + 1) % N_CLUS, peer)
    slot_place = jnp.where(forced, SLOT_COUNT - 1, slot_place)
    remote = remote | forced
    return jnp.where(remote, MESH_DEV + peer * SLOT_COUNT + slot_place, local_mesh).astype(jnp.int32)


def draw_admissible(key, part):
    band_width = TILES // FAR_COUNT
    band_offset = jax.random.randint(jax.random.fold_in(key, 41), (TILES, FAR_COUNT), 1, band_width)
    tile_rows = jnp.arange(TILES, dtype=jnp.int32)[:, None]
    band_index = jnp.arange(FAR_COUNT, dtype=jnp.int32)[None, :]
    return ((tile_rows + band_index * band_width + band_offset) % TILES).astype(jnp.int32)


def draw_port_mesh(key, part):
    return jax.random.permutation(jax.random.fold_in(key, 51), MESHES)[:PORT_COUNT].astype(jnp.int32)


def plant(result, rng, smallest, largest):
    place = [jax.random.randint(jax.random.fold_in(rng, axis), (), 0, length) for axis, length in enumerate(result.shape)]
    longest = result.shape.index(max(result.shape))
    beside = place[:longest] + [(place[longest] + 1) % result.shape[longest]] + place[longest + 1:]
    return result.at[tuple(place)].set(smallest).at[tuple(beside)].set(largest)


def block_levels(key, extent, cuts, least, largest):
    factor_of, own = 1.0, jax.random.fold_in(key, 6)
    for dim, shards_of in cuts:
        steps = jnp.exp(jax.random.uniform(jax.random.fold_in(own, dim), (shards_of,), jnp.float32, least / len(cuts), largest / len(cuts)))
        factor_of = factor_of * jnp.repeat(steps, extent[dim] // shards_of).reshape([-1 if axis == dim else 1 for axis in range(len(extent))])
    return factor_of


def scatter_about(own_key, dims, spread, limit, pieces=(), kind=jnp.bfloat16):
    result = jax.random.normal(own_key, dims, jnp.float32) * spread
    if len(pieces) > 0:
        result = block_levels(own_key, dims, pieces, -0.22, 0.18) * result
    return jnp.clip(result, min=-limit, max=limit).astype(kind)


def setup_inputs(seed: int = 0, part: int = 0) -> dict:
    seeds = jax.random.split(jax.random.key(seed), 14)
    part_keys = jax.random.split(jax.random.fold_in(seeds[13], part), 14)
    return {
        "mesh_current": scatter_about(part_keys[0], (2, MESHES), 1.0, 6.0, ((1, 16),), jnp.float32),
        "branch_entry": draw_branch_entry(jax.random.fold_in(jax.random.fold_in(seeds[13], part), 71), part),
        "branch_sign": plant(jax.random.randint(part_keys[2], (ENTRIES, BRANCHES), 0, 2), jax.random.fold_in(part_keys[2], 1), 0, 1).astype(jnp.int32),
        "need_slots": draw_need_slots(jax.random.fold_in(jax.random.fold_in(seeds[13], part), 71), part),
        "resistance": jnp.clip(jnp.exp(math.log(3.0) - 2.3025851 * jax.random.uniform(part_keys[4], (BRANCHES,), jnp.float32) ** block_levels(part_keys[4], (BRANCHES,), ((0, 16),), -0.2, 0.2)), 0.3, 3.0),
        "near_blocks": scatter_about(part_keys[5], (TILES, NEAR_COUNT, TILE_SIZE, TILE_SIZE), (NEAR_COUNT * TILE_SIZE) ** -0.5, 0.25, ((0, 16),)),
        "near_source": plant(jax.random.randint(part_keys[6], (TILES, NEAR_COUNT), 0, TILE_DEV), jax.random.fold_in(part_keys[6], 1), 0, TILE_DEV - 1).astype(jnp.int32),
        "basis_in": scatter_about(part_keys[7], (TILES, FAR_RANK, TILE_SIZE), TILE_SIZE ** -0.5, 0.5, ((0, 16),)),
        "coupling": scatter_about(part_keys[8], (TILES, FAR_COUNT, FAR_RANK, FAR_RANK), (FAR_COUNT * FAR_RANK) ** -0.5, 0.25, ((0, 16),)),
        "basis_out": scatter_about(part_keys[9], (TILES, FAR_RANK, TILE_SIZE), FAR_RANK ** -0.5, 1.0, ((0, 16),)),
        "admissible": draw_admissible(jax.random.fold_in(jax.random.fold_in(seeds[13], part), 71), part),
        "port_mesh": draw_port_mesh(jax.random.fold_in(jax.random.fold_in(seeds[13], part), 71), part),
        "port_coupling": scatter_about(seeds[12], (2, PORT_COUNT, PORT_COUNT), PORT_COUNT ** -0.5, 0.75, (), jnp.float32),
    }


def near_part(block):
    blocks, source, inputs = block
    gathered = inputs[:, source]
    return jnp.einsum("tkij,ctkj->cti", blocks.astype(jnp.float32), gathered.astype(jnp.float32))


def segment_one(values, segment_ids):
    return jax.ops.segment_sum(values, segment_ids, num_segments=MESHES)


def reference(mesh_current, branch_entry, branch_sign, need_slots, resistance, near_blocks, near_source, basis_in, coupling, basis_out, admissible, port_mesh, port_coupling):
    devices = jnp.arange(N_CLUS, dtype=jnp.int32)
    table_width = MESH_DEV + N_CLUS * SLOT_COUNT
    needed = jnp.maximum(need_slots, 0).reshape(N_CLUS, N_CLUS * SLOT_COUNT)
    owner_base = jnp.repeat(devices * MESH_DEV, SLOT_COUNT)
    slot_mesh = needed + owner_base[None, :]
    own_mesh = devices[:, None] * MESH_DEV + jnp.arange(MESH_DEV, dtype=jnp.int32)[None, :]
    lookup_table = jnp.concatenate([own_mesh, slot_mesh], axis=1).reshape(-1)
    entries = branch_entry.reshape(ENTRIES, N_CLUS, BRANCH_DEV)
    flat_index = (devices[None, :, None] * table_width + entries).astype(jnp.int32)
    incident = lookup_table[flat_index].reshape(ENTRIES, BRANCHES)
    orient = (2 * branch_sign - 1).astype(jnp.float32)
    branch_current = jnp.sum(orient[None] * mesh_current[:, incident], axis=1)
    branch_input = branch_current.astype(jnp.bfloat16).reshape(2, TILES, TILE_SIZE)
    by_device = jnp.transpose(branch_input.reshape(2, N_CLUS, TILE_DEV, TILE_SIZE), (1, 0, 2, 3))
    near = lax.map(near_part, (near_blocks.reshape(N_CLUS, TILE_DEV, NEAR_COUNT, TILE_SIZE, TILE_SIZE), near_source.reshape(N_CLUS, TILE_DEV, NEAR_COUNT), by_device))
    near_field = jnp.transpose(near, (1, 0, 2, 3)).reshape(2, TILES, TILE_SIZE)
    far_coeff = jnp.einsum("tri,cti->ctr", basis_in.astype(jnp.float32), branch_input.astype(jnp.float32)).astype(jnp.bfloat16)
    picked = far_coeff[:, admissible]
    far_mixed = jnp.einsum("tkrq,ctkq->ctr", coupling.astype(jnp.float32), picked.astype(jnp.float32)).astype(jnp.bfloat16)
    far_field = jnp.einsum("tri,ctr->cti", basis_out.astype(jnp.float32), far_mixed.astype(jnp.float32))
    reactive = (near_field + far_field).reshape(2, BRANCHES)
    branch_voltage = resistance[None, :] * branch_current + jnp.stack([-reactive[1], reactive[0]])
    contributions = (orient[None] * branch_voltage[:, None, :]).reshape(2, -1)
    mesh_voltage = jax.vmap(segment_one, in_axes=(0, None))(contributions, incident.reshape(-1))
    port_current = mesh_current[:, port_mesh]
    high = lax.Precision.HIGHEST
    real_part = jnp.dot(port_coupling[0], port_current[0], precision=high) - jnp.dot(port_coupling[1], port_current[1], precision=high)
    imag_part = jnp.dot(port_coupling[0], port_current[1], precision=high) + jnp.dot(port_coupling[1], port_current[0], precision=high)
    mesh_voltage = mesh_voltage.at[:, port_mesh].add(jnp.stack([real_part, imag_part]))
    return mesh_voltage
```

```python
import functools

import jax
import jax.numpy as jnp
from jax import lax
from jax.experimental import pallas as pl
from jax.experimental.pallas import tpu as pltpu
from jax.sharding import PartitionSpec as P

LANES = 128
GROUP = 8
LOOK_CHUNK = 2048
SUM_CHUNK = 2048
VMEM_LIMIT = 60 * 1024 * 1024
NT = (((1,), (1,)), ((), ()))
TN = (((0,), (0,)), ((), ()))


def greet(peers):
    me = lax.axis_index("clus")
    barrier = pltpu.get_barrier_semaphore()
    for step in range(1, peers):
        pl.semaphore_signal(
            barrier,
            inc=1,
            device_id={"clus": lax.rem(me + step, peers)},
            device_id_type=pl.DeviceIdType.MESH,
        )
    return lambda: pl.semaphore_wait(barrier, peers - 1)


def push(peers, phase, source_at, target_at, send_sem, recv_sem):
    me = lax.axis_index("clus")
    copies = []
    for step in range(1, peers):
        peer = lax.rem(me + step, peers)
        copy = pltpu.make_async_remote_copy(
            src_ref=source_at(step, peer),
            dst_ref=target_at(step, me),
            send_sem=send_sem.at[phase, step],
            recv_sem=recv_sem.at[phase, step],
            device_id={"clus": peer},
            device_id_type=pl.DeviceIdType.MESH,
        )
        copy.start()
        copies.append(copy)

    def arrive():
        for copy in copies:
            copy.wait_recv()

    def leave():
        for copy in copies:
            copy.wait_send()

    return arrive, leave


def one_hot(rows, index):
    match = lax.broadcasted_iota(jnp.int32, (rows, index.shape[1]), 0) == index
    return jnp.where(match, 1.0, 0.0).astype(jnp.bfloat16)


def pick(tables, low, row):
    sub = lax.broadcasted_iota(jnp.int32, (GROUP, LANES), 0)
    lanes = jnp.broadcast_to(low, (GROUP, LANES))
    gap = jnp.broadcast_to(row, (GROUP, LANES)) - sub
    total = [0.0, 0.0]
    for block in range(len(tables[0])):
        match = gap == block * GROUP
        for c in range(2):
            found = jnp.take_along_axis(
                tables[c][block], lanes, axis=1, mode="promise_in_bounds"
            )
            total[c] += jnp.where(match, found, 0.0)
    return total


def fold(value):
    return jnp.sum(value, axis=0, keepdims=True)


def blocks_of(table):
    return [table[start : start + GROUP] for start in range(0, table.shape[0], GROUP)]


def branch_flows(tables, first_row, add, entry_ref, sign_ref, flow_ref):
    groups = LOOK_CHUNK // (GROUP * LANES)

    @pl.loop(0, entry_ref.shape[1] // LOOK_CHUNK)
    def _(step):
        for group in range(groups):
            rows = [[], []]
            for j in range(GROUP):
                start = step * LOOK_CHUNK + (group * GROUP + j) * LANES
                columns = pl.ds(pl.multiple_of(start, LANES), LANES)
                total = [0.0, 0.0]
                for k in range(entry_ref.shape[0]):
                    entry = entry_ref[k : k + 1, columns]
                    orient = (2 * sign_ref[k : k + 1, columns] - 1).astype(jnp.float32)
                    found = pick(tables, entry & (LANES - 1), (entry >> 7) - first_row)
                    total = [total[c] + orient * found[c] for c in range(2)]
                for c in range(2):
                    rows[c].append(fold(total[c]))
            for c in range(2):
                start = (step * groups + group) * 2 * GROUP + c * GROUP
                place = pl.ds(pl.multiple_of(start, GROUP), GROUP)
                made = jnp.concatenate(rows[c], axis=0)
                flow_ref[place, :] = flow_ref[place, :] + made if add else made


def spread_sums(values, index, first_row, rows):
    low, row = index & (LANES - 1), (index >> 7) - first_row
    mask = lax.broadcasted_iota(jnp.int32, (rows, index.shape[1]), 0) == row
    high = [value.astype(jnp.bfloat16).astype(jnp.float32) for value in values]
    parts = high + [value - top for value, top in zip(values, high)]
    spread = [jnp.where(mask, part, 0.0).astype(jnp.bfloat16) for part in parts]
    return jnp.concatenate(spread, axis=0), one_hot(LANES, low)


def add_up(spread, hot):
    made = lax.dot_general(spread, hot, NT, preferred_element_type=jnp.float32)
    half = made.shape[0] // 2
    return made[:half] + made[half:]


def collect(entry_ref, sign_ref, voltage_ref, first_row, rows, o_ref):
    o_ref[...] = jnp.zeros_like(o_ref)
    groups = SUM_CHUNK // (GROUP * LANES)

    @pl.loop(0, entry_ref.shape[1] // SUM_CHUNK)
    def _(step):
        columns = pl.ds(pl.multiple_of(step * SUM_CHUNK, SUM_CHUNK), SUM_CHUNK)
        voltage = []
        for c in range(2):
            lines = []
            for group in range(groups):
                start = (step * groups + group) * 2 * GROUP + c * GROUP
                tile = voltage_ref[pl.ds(pl.multiple_of(start, GROUP), GROUP), :]
                lines += [tile[j : j + 1] for j in range(GROUP)]
            voltage.append(jnp.concatenate(lines, axis=1))
        made = []
        for k in range(entry_ref.shape[0]):
            orient = (2 * sign_ref[k : k + 1, columns] - 1).astype(jnp.float32)
            values = [orient * value for value in voltage]
            made.append(spread_sums(values, entry_ref[k : k + 1, columns], first_row, rows))
        o_ref[...] += add_up(
            jnp.concatenate([spread for spread, _ in made], axis=1),
            jnp.concatenate([hot for _, hot in made], axis=1),
        )


def far_coefficients(basis_ref, flow_ref, o_ref):
    flows = flow_ref[...].astype(jnp.bfloat16)
    count = flows.shape[0]
    tile_dev = count // 2
    rank = basis_ref.shape[0] // tile_dev
    lane = lax.broadcasted_iota(jnp.int32, (rank, count), 1)
    tile = (lane >> 4) * GROUP + (lane & (GROUP - 1))
    total = jnp.zeros((rank, count), jnp.float32)
    for start in range(0, tile_dev, GROUP):
        crossed = lax.dot_general(
            basis_ref[start * rank : (start + GROUP) * rank, :],
            flows,
            NT,
            preferred_element_type=jnp.float32,
        )
        for j in range(GROUP):
            total = jnp.where(tile == start + j, crossed[j * rank : (j + 1) * rank], total)
    o_ref[...] = total.astype(jnp.bfloat16)


def near_choice(source_ref, hot_ref):
    near_count, tile_dev = source_ref.shape
    count = 2 * tile_dev
    lane = lax.broadcasted_iota(jnp.int32, (tile_dev, count), 1)
    tile = (lane >> 4) * GROUP + (lane & (GROUP - 1))
    widen = lax.broadcasted_iota(jnp.int32, (tile_dev, count), 0) == tile
    source = jnp.dot(
        source_ref[...].astype(jnp.float32).astype(jnp.bfloat16),
        jnp.where(widen, 1.0, 0.0).astype(jnp.bfloat16),
        preferred_element_type=jnp.float32,
    ).astype(jnp.int32)
    part = lax.broadcasted_iota(jnp.int32, (near_count, count), 1) & GROUP
    place = (source >> 3) * 2 * GROUP + part + (source & (GROUP - 1))
    for k in range(near_count):
        hot = jnp.where(
            lax.broadcasted_iota(jnp.int32, (count, count), 0) == place[k : k + 1], 1.0, 0.0
        )
        hot_ref[k] = hot.T.astype(jnp.bfloat16)


def near_work(flow_ref, hot_ref, blocks_ref, picked_ref, near_ref):
    near_count = blocks_ref.shape[1]
    flows = flow_ref[...].astype(jnp.bfloat16)
    for k in range(near_count):
        picked_ref[:, k * LANES : (k + 1) * LANES] = jnp.dot(
            hot_ref[k], flows, preferred_element_type=jnp.float32
        ).astype(jnp.bfloat16)

    @pl.loop(0, blocks_ref.shape[0] // GROUP)
    def _(step):
        place = pl.ds(pl.multiple_of(step * 2 * GROUP, 2 * GROUP), 2 * GROUP)
        source = picked_ref[place, :]
        row = lax.broadcasted_iota(jnp.int32, (2 * GROUP, LANES), 0) & (GROUP - 1)
        total = jnp.zeros((2 * GROUP, LANES), jnp.float32)
        for j in range(GROUP):
            block = jnp.concatenate(
                [blocks_ref[step * GROUP + j, k] for k in range(near_count)], axis=1
            )
            made = lax.dot_general(source, block, NT, preferred_element_type=jnp.float32)
            total = jnp.where(row == j, made, total)
        near_ref[place, :] = total


def far_choice(peers, admissible_ref, hot_ref):
    far_count, tile_dev = admissible_ref.shape
    tiles = peers * tile_dev
    band = tiles // far_count
    first = lax.axis_index("clus") * tile_dev
    entry = lax.broadcasted_iota(jnp.int32, (far_count, tile_dev), 0)
    place = admissible_ref[...] - first - entry * band
    place = jnp.where(place < 0, place + tiles, place)
    place = jnp.where(place < 0, place + tiles, place)
    place = jnp.concatenate([place, place], axis=1)
    owner, tile = place // tile_dev, place % tile_dev
    lane = lax.broadcasted_iota(jnp.int32, (far_count, 2 * tile_dev), 1)
    part = jnp.where(lane < tile_dev, 0, GROUP)
    line = owner * 2 * tile_dev + (tile >> 3) * 2 * GROUP + part + (tile & (GROUP - 1))
    for k in range(far_count):
        hot_ref[k] = one_hot(hot_ref.shape[1], line[k : k + 1])


def far_mix(peers, coeff_ref, hot_ref, coupling_ref, picked_ref, mixed_ref):
    far_count, rank, _, tile_dev = coupling_ref.shape
    span = hot_ref.shape[1] // (2 * tile_dev)
    stride = peers // far_count
    for k in range(far_count):
        held = jnp.concatenate(
            [coeff_ref[(k * stride + j) % peers] for j in range(span)], axis=1
        )
        found = jnp.dot(held, hot_ref[k], preferred_element_type=jnp.float32)
        for c in range(2):
            picked_ref[c, k, :, :tile_dev] = found[:, c * tile_dev : (c + 1) * tile_dev]

    @pl.loop(0, rank)
    def _(r):
        total = [0.0, 0.0]
        for k in range(far_count):
            block = coupling_ref[k, r].astype(jnp.float32)
            total = [total[c] + block * picked_ref[c, k, :, :tile_dev] for c in range(2)]
        for c in range(2):
            mixed_ref[c, pl.ds(r, 1), :] = fold(total[c])


def voltages(mixed_ref, basis_ref, near_ref, flow_ref, resistance_ref, voltage_ref):
    rank, tile_dev = mixed_ref.shape[1:]
    width = GROUP * rank
    repeat = lax.broadcasted_iota(jnp.int32, (rank, width), 1) % rank
    repeat = jnp.where(
        lax.broadcasted_iota(jnp.int32, (rank, width), 0) == repeat, 1.0, 0.0
    ).astype(jnp.bfloat16)
    wide = [
        lax.dot_general(
            mixed_ref[c].T.astype(jnp.bfloat16), repeat, (((1,), (0,)), ((), ())),
            preferred_element_type=jnp.float32,
        )
        for c in range(2)
    ]
    mask = lax.broadcasted_iota(jnp.int32, (GROUP, width), 1) // rank
    mask = mask == lax.broadcasted_iota(jnp.int32, (GROUP, width), 0)
    for group in range(tile_dev // GROUP):
        own = slice(group * GROUP, (group + 1) * GROUP)
        mixed = jnp.concatenate([jnp.where(mask, wide[c][own], 0.0) for c in range(2)], axis=0)
        far = jnp.dot(
            mixed.astype(jnp.bfloat16),
            basis_ref[group * width : (group + 1) * width, :],
            preferred_element_type=jnp.float32,
        )
        place = slice(group * 2 * GROUP, (group + 1) * 2 * GROUP)
        reactive = near_ref[place, :] + far
        flow = flow_ref[place, :]
        resistance = resistance_ref[own, :]
        voltage_ref[place, :] = jnp.concatenate(
            [
                resistance * flow[:GROUP] - reactive[GROUP:],
                resistance * flow[GROUP:] + reactive[:GROUP],
            ],
            axis=0,
        )


def port_sums(current, z_ref):
    products = [
        lax.dot_general(
            current,
            z_ref[part],
            NT,
            precision=lax.Precision.HIGHEST,
            preferred_element_type=jnp.float32,
        )
        for part in range(2)
    ]
    return [products[0][0:1] - products[1][1:2], products[0][1:2] + products[1][0:1]]


def whole_kernel(
    peers,
    need_hbm,
    current_hbm,
    port_hbm,
    entry_hbm,
    sign_hbm,
    basis_in_hbm,
    source_hbm,
    blocks_hbm,
    admissible_hbm,
    coupling_hbm,
    basis_out_hbm,
    resistance_hbm,
    z_hbm,
    o_ref,
    need_ref,
    current_ref,
    port_ref,
    entry_ref,
    sign_ref,
    basis_in_ref,
    source_ref,
    blocks_ref,
    admissible_ref,
    coupling_ref,
    basis_out_ref,
    resistance_ref,
    z_ref,
    asked_ref,
    reply_ref,
    answer_ref,
    flow_ref,
    coeff_ref,
    near_hot_ref,
    near_picked_ref,
    near_ref,
    far_hot_ref,
    picked_ref,
    mixed_ref,
    voltage_ref,
    remote_ref,
    local_ref,
    slots_ref,
    arrived_ref,
    send_sem,
    recv_sem,
    load_sem,
):
    me = lax.axis_index("clus")
    met = greet(peers)
    pairs = [
        (need_hbm, need_ref),
        (current_hbm, current_ref),
        (entry_hbm, entry_ref),
        (sign_hbm, sign_ref),
        (port_hbm, port_ref),
        (source_hbm, source_ref),
        (admissible_hbm, admissible_ref),
        (basis_in_hbm, basis_in_ref),
        (blocks_hbm, blocks_ref),
        (coupling_hbm, coupling_ref),
        (basis_out_hbm, basis_out_ref),
        (resistance_hbm, resistance_ref),
        (z_hbm, z_ref),
    ]
    loads = [
        pltpu.make_async_copy(source, target, load_sem.at[i])
        for i, (source, target) in enumerate(pairs)
    ]
    for load in loads:
        load.start()
    (
        need_load,
        current_load,
        entry_load,
        sign_load,
        port_load,
        source_load,
        admissible_load,
        basis_in_load,
        blocks_load,
        coupling_load,
        basis_out_load,
        resistance_load,
        z_load,
    ) = loads
    sems = (send_sem, recv_sem)
    mesh_rows = current_ref.shape[0]
    ports = port_ref.shape[1]
    asked_ref[me] = jnp.full(asked_ref.shape[1:], -1, jnp.int32)
    need_load.wait()
    met()
    arrive, leave_need = push(
        peers,
        0,
        lambda step, peer: need_ref.at[peer],
        lambda step, own: asked_ref.at[own],
        *sems,
    )
    current_load.wait()
    entry_load.wait()
    sign_load.wait()
    own_tables = [blocks_of(current_ref[:, c, :]) for c in range(2)]
    branch_flows(own_tables, 0, False, entry_ref, sign_ref, flow_ref)
    port_load.wait()
    port = jnp.concatenate(
        [port_ref[...], jnp.full((1, LANES - ports), -1, jnp.int32)], axis=1
    ) - me * (mesh_rows * LANES)
    port_row = port >> 7
    held = pick(own_tables, port & (LANES - 1), port_row)
    port_current = [fold(held[c]) for c in range(2)]
    arrive()
    for p in range(peers):
        asked = asked_ref[p]
        found = pick(own_tables, asked & (LANES - 1), asked >> 7)
        reply_ref[p] = jnp.concatenate([fold(found[c]) for c in range(2)] + port_current, axis=0)
    arrive, leave_reply = push(
        peers,
        1,
        lambda step, peer: reply_ref.at[peer],
        lambda step, own: answer_ref.at[own],
        *sems,
    )
    answer_ref[me] = jnp.concatenate([jnp.zeros((2, LANES), jnp.float32)] + port_current, axis=0)
    source_load.wait()
    near_choice(source_ref, near_hot_ref)
    admissible_load.wait()
    far_choice(peers, admissible_ref, far_hot_ref)
    basis_in_load.wait()
    arrive()
    tables = [blocks_of(answer_ref[:, c, :]) for c in range(2)]
    branch_flows(tables, mesh_rows, True, entry_ref, sign_ref, flow_ref)
    far_coefficients(basis_in_ref, flow_ref, coeff_ref.at[0])
    arrive, leave_coeff = push(
        peers,
        2,
        lambda step, peer: coeff_ref.at[0],
        lambda step, own: coeff_ref.at[peers - step],
        *sems,
    )
    blocks_load.wait()
    near_work(flow_ref, near_hot_ref, blocks_ref, near_picked_ref, near_ref)
    coupling_load.wait()
    basis_out_load.wait()
    resistance_load.wait()
    arrive()
    far_mix(peers, coeff_ref, far_hot_ref, coupling_ref, picked_ref, mixed_ref)
    voltages(mixed_ref, basis_out_ref, near_ref, flow_ref, resistance_ref, voltage_ref)
    collect(entry_ref, sign_ref, voltage_ref, mesh_rows, peers, remote_ref)
    for c in range(2):
        slots_ref[:, c, :] = remote_ref[c * peers : (c + 1) * peers, :]
    arrive, leave_slots = push(
        peers,
        3,
        lambda step, peer: slots_ref.at[peer],
        lambda step, own: arrived_ref.at[own],
        *sems,
    )
    arrived_ref[me] = jnp.zeros(arrived_ref.shape[1:], jnp.float32)
    collect(entry_ref, sign_ref, voltage_ref, 0, mesh_rows, local_ref)
    z_load.wait()
    current = answer_ref[0]
    for p in range(1, peers):
        current = current + answer_ref[p]
    port_voltage = [
        jnp.concatenate([value, jnp.zeros((1, LANES - ports), jnp.float32)], axis=1)
        for value in port_sums(current[2:4, :ports], z_ref)
    ]
    asked = jnp.concatenate([asked_ref[p] for p in range(peers)] + [port], axis=1)
    for leave in (leave_need, leave_reply, leave_coeff):
        leave()
    arrive()
    values = [
        jnp.concatenate([arrived_ref[p, c : c + 1] for p in range(peers)] + [port_voltage[c]], axis=1)
        for c in range(2)
    ]
    total = local_ref[...] + add_up(*spread_sums(values, asked, 0, mesh_rows))
    for c in range(2):
        o_ref[:, c, :] = total[c * mesh_rows : (c + 1) * mesh_rows]
    leave_slots()


def per_device(
    mesh_current,
    branch_entry,
    branch_sign,
    need_slots,
    resistance,
    near_blocks,
    near_source,
    basis_in,
    coupling,
    basis_out,
    admissible,
    port_mesh,
    port_coupling,
):
    peers = lax.axis_size("clus")
    mesh_dev = mesh_current.shape[1]
    tile_dev, near_count, tile_width = near_blocks.shape[:3]
    rank = basis_in.shape[1]
    mesh_rows = mesh_dev // LANES
    far_count = admissible.shape[1]
    band = peers * tile_dev // far_count
    span = (band + tile_dev - 2) // tile_dev + 1
    operands = [
        need_slots[:, None, :],
        mesh_current.reshape(2, mesh_rows, LANES).transpose(1, 0, 2),
        port_mesh[None, :],
        branch_entry,
        branch_sign,
        basis_in.reshape(tile_dev * rank, tile_width),
        near_source.T,
        near_blocks,
        admissible.T,
        coupling.transpose(1, 2, 3, 0),
        basis_out.reshape(tile_dev * rank, tile_width),
        resistance.reshape(tile_dev, tile_width),
        port_coupling,
    ]
    f32, bf16 = jnp.float32, jnp.bfloat16
    tiles = pltpu.VMEM((2 * tile_dev, LANES), f32)
    message = pltpu.VMEM((peers, 2, LANES), f32)
    made = pl.pallas_call(
        functools.partial(whole_kernel, peers),
        out_shape=jax.ShapeDtypeStruct((mesh_rows, 2, LANES), f32),
        in_specs=[pl.BlockSpec(memory_space=pltpu.HBM)] * len(operands),
        out_specs=pl.BlockSpec(memory_space=pltpu.VMEM),
        scratch_shapes=[pltpu.VMEM(x.shape, x.dtype) for x in operands]
        + [
            pltpu.VMEM((peers, 1, LANES), jnp.int32),
            pltpu.VMEM((peers, 4, LANES), f32),
            pltpu.VMEM((peers, 4, LANES), f32),
            tiles,
            pltpu.VMEM((peers, rank, 2 * tile_dev), bf16),
            pltpu.VMEM((near_count, 2 * tile_dev, 2 * tile_dev), bf16),
            pltpu.VMEM((2 * tile_dev, near_count * LANES), bf16),
            tiles,
            pltpu.VMEM((far_count, span * 2 * tile_dev, 2 * tile_dev), bf16),
            pltpu.VMEM((2, far_count, rank, LANES), f32),
            pltpu.VMEM((2, rank, tile_dev), f32),
            tiles,
            pltpu.VMEM((2 * peers, LANES), f32),
            pltpu.VMEM((2 * mesh_rows, LANES), f32),
            message,
            message,
            pltpu.SemaphoreType.DMA((4, peers)),
            pltpu.SemaphoreType.DMA((4, peers)),
            pltpu.SemaphoreType.DMA((len(operands),)),
        ],
        compiler_params=pltpu.CompilerParams(
            collective_id=0, has_side_effects=True, vmem_limit_bytes=VMEM_LIMIT
        ),
    )(*operands)
    return made.transpose(1, 0, 2).reshape(2, mesh_dev)


def solution(mesh):
    both = ("groups", "clus")
    in_specs = (
        P(None, both),
        P(None, both),
        P(None, both),
        P(both, None),
        P(both),
        P(both, None, None, None),
        P(both, None),
        P(both, None, None),
        P(both, None, None, None),
        P(both, None, None),
        P(both, None),
        P("groups"),
        P(),
    )
    return jax.shard_map(
        per_device, mesh=mesh, in_specs=in_specs, out_specs=P(None, both), check_vma=False
    )
```

```python
import functools

import jax
import jax.numpy as jnp
from jax import lax
from jax.experimental import pallas as pl
from jax.experimental.pallas import tpu as pltpu
from jax.sharding import PartitionSpec as P

LANES = 128
GROUP = 8
LOCAL_CHUNK = 2048
REMOTE_CHUNK = 8192
HOT_CHUNK = 1024
MIX_STEP = 4
VMEM_LIMIT = 60 * 1024 * 1024
NT = (((1,), (1,)), ((), ()))


def greet(peers):
    me = lax.axis_index("clus")
    barrier = pltpu.get_barrier_semaphore()
    for step in range(1, peers):
        pl.semaphore_signal(
            barrier,
            inc=1,
            device_id={"clus": lax.rem(me + step, peers)},
            device_id_type=pl.DeviceIdType.MESH,
        )
    return lambda: pl.semaphore_wait(barrier, peers - 1)


def push(peers, phase, source_at, target_at, send_sem, recv_sem):
    me = lax.axis_index("clus")
    copies = []
    for step in range(1, peers):
        peer = lax.rem(me + step, peers)
        copy = pltpu.make_async_remote_copy(
            src_ref=source_at(step, peer),
            dst_ref=target_at(step, me),
            send_sem=send_sem.at[phase, step],
            recv_sem=recv_sem.at[phase, step],
            device_id={"clus": peer},
            device_id_type=pl.DeviceIdType.MESH,
        )
        copy.start()
        copies.append(copy)

    def arrive():
        for copy in copies:
            copy.wait_recv()

    def leave():
        for copy in copies:
            copy.wait_send()

    return arrive, leave


def one_hot(rows, index):
    match = lax.broadcasted_iota(jnp.int32, (rows, index.shape[1]), 0) == index
    return jnp.where(match, 1.0, 0.0).astype(jnp.bfloat16)


def pick(tables, low, row):
    sub = lax.broadcasted_iota(jnp.int32, (GROUP, LANES), 0)
    lanes = jnp.broadcast_to(low, (GROUP, LANES))
    gap = jnp.broadcast_to(row, (GROUP, LANES)) - sub
    total = [0.0, 0.0]
    for block in range(len(tables[0])):
        match = gap == block * GROUP
        for c in range(2):
            found = jnp.take_along_axis(
                tables[c][block], lanes, axis=1, mode="promise_in_bounds"
            )
            total[c] += jnp.where(match, found, 0.0)
    return total


def fold(value):
    return jnp.sum(value, axis=0, keepdims=True)


def blocks_of(table):
    return [table[start : start + GROUP] for start in range(0, table.shape[0], GROUP)]


def branch_flows(tables, first_row, add, chunk, entry_ref, sign_ref, flow_ref):
    chunk = min(chunk, entry_ref.shape[1])
    groups = chunk // (GROUP * LANES)

    @pl.loop(0, entry_ref.shape[1] // chunk)
    def _(step):
        for group in range(groups):
            rows = [[], []]
            for j in range(GROUP):
                start = step * chunk + (group * GROUP + j) * LANES
                columns = pl.ds(pl.multiple_of(start, LANES), LANES)
                total = [0.0, 0.0]
                for k in range(entry_ref.shape[0]):
                    entry = entry_ref[k : k + 1, columns]
                    orient = (2 * sign_ref[k : k + 1, columns] - 1).astype(jnp.float32)
                    found = pick(tables, entry & (LANES - 1), (entry >> 7) - first_row)
                    total = [total[c] + orient * found[c] for c in range(2)]
                for c in range(2):
                    rows[c].append(fold(total[c]))
            for c in range(2):
                start = (step * groups + group) * 2 * GROUP + c * GROUP
                place = pl.ds(pl.multiple_of(start, GROUP), GROUP)
                made = jnp.concatenate(rows[c], axis=0)
                flow_ref[place, :] = flow_ref[place, :] + made if add else made


def signed_hot(entry_ref, sign_ref, hot_ref):
    @pl.loop(0, entry_ref.shape[1] // HOT_CHUNK)
    def _(step):
        columns = pl.ds(pl.multiple_of(step * HOT_CHUNK, HOT_CHUNK), HOT_CHUNK)
        for k in range(entry_ref.shape[0]):
            orient = (2 * sign_ref[k : k + 1, columns] - 1).astype(jnp.float32)
            low = entry_ref[k : k + 1, columns] & (LANES - 1)
            match = lax.broadcasted_iota(jnp.int32, (LANES, HOT_CHUNK), 0) == low
            hot_ref[k, :, columns] = jnp.where(match, orient, 0.0).astype(jnp.bfloat16)


def halves(value):
    high = value.astype(jnp.bfloat16).astype(jnp.float32)
    return high, value - high


def spread_over(parts, row, rows):
    mask = lax.broadcasted_iota(jnp.int32, (rows, row.shape[1]), 0) == row
    return jnp.concatenate(
        [jnp.where(mask, part, 0.0).astype(jnp.bfloat16) for part in parts], axis=0
    )


def add_up(hot, spread):
    return lax.dot_general(hot, spread, NT, preferred_element_type=jnp.float32)


def join(made):
    turned = made.T
    half = turned.shape[0] // 2
    return turned[:half] + turned[half:]


def collect(entry_ref, hot_ref, voltage_ref, first_row, rows, chunk):
    count = entry_ref.shape[1]
    chunk = min(chunk, count)
    groups = chunk // (GROUP * LANES)

    def body(step, total):
        columns = pl.ds(pl.multiple_of(step * chunk, chunk), chunk)
        parts = []
        for part in range(2):
            for c in range(2):
                lines = []
                for group in range(groups):
                    start = (step * groups + group) * 2 * GROUP + c * GROUP
                    tile = voltage_ref[part, pl.ds(pl.multiple_of(start, GROUP), GROUP), :]
                    lines += [tile[j : j + 1] for j in range(GROUP)]
                parts.append(jnp.concatenate(lines, axis=1))
        for k in range(entry_ref.shape[0]):
            row = (entry_ref[k : k + 1, columns] >> 7) - first_row
            total += add_up(hot_ref[k, :, columns], spread_over(parts, row, rows))
        return total

    total = jnp.zeros((LANES, 4 * rows), jnp.float32)
    if count == chunk:
        return join(body(0, total))
    return join(lax.fori_loop(0, count // chunk, body, total))


def far_coefficients(basis_ref, flow_ref, o_ref):
    flows = flow_ref[...].astype(jnp.bfloat16)
    count = flows.shape[0]
    tile_dev = count // 2
    rank = basis_ref.shape[0] // tile_dev
    lane = lax.broadcasted_iota(jnp.int32, (rank, count), 1)
    tile = (lane >> 4) * GROUP + (lane & (GROUP - 1))
    total = jnp.zeros((rank, count), jnp.float32)
    for start in range(0, tile_dev, GROUP):
        crossed = lax.dot_general(
            basis_ref[start * rank : (start + GROUP) * rank, :],
            flows,
            NT,
            preferred_element_type=jnp.float32,
        )
        for j in range(GROUP):
            total = jnp.where(tile == start + j, crossed[j * rank : (j + 1) * rank], total)
    o_ref[...] = total.astype(jnp.bfloat16)


def near_choice(source_ref, hot_ref):
    near_count, tile_dev = source_ref.shape
    count = 2 * tile_dev
    lane = lax.broadcasted_iota(jnp.int32, (tile_dev, count), 1)
    tile = (lane >> 4) * GROUP + (lane & (GROUP - 1))
    widen = lax.broadcasted_iota(jnp.int32, (tile_dev, count), 0) == tile
    source = jnp.dot(
        source_ref[...].astype(jnp.float32).astype(jnp.bfloat16),
        jnp.where(widen, 1.0, 0.0).astype(jnp.bfloat16),
        preferred_element_type=jnp.float32,
    ).astype(jnp.int32)
    part = lax.broadcasted_iota(jnp.int32, (near_count, count), 1) & GROUP
    place = (source >> 3) * 2 * GROUP + part + (source & (GROUP - 1))
    for k in range(near_count):
        hot = jnp.where(
            lax.broadcasted_iota(jnp.int32, (count, count), 0) == place[k : k + 1], 1.0, 0.0
        )
        hot_ref[k] = hot.T.astype(jnp.bfloat16)


def near_work(flow_ref, hot_ref, blocks_ref, picked_ref, near_ref):
    near_count = blocks_ref.shape[1]
    flows = flow_ref[...].astype(jnp.bfloat16)
    for k in range(near_count):
        picked_ref[:, k * LANES : (k + 1) * LANES] = jnp.dot(
            hot_ref[k], flows, preferred_element_type=jnp.float32
        ).astype(jnp.bfloat16)

    @pl.loop(0, blocks_ref.shape[0] // GROUP)
    def _(step):
        place = pl.ds(pl.multiple_of(step * 2 * GROUP, 2 * GROUP), 2 * GROUP)
        source = picked_ref[place, :]
        row = lax.broadcasted_iota(jnp.int32, (2 * GROUP, LANES), 0) & (GROUP - 1)
        total = jnp.zeros((2 * GROUP, LANES), jnp.float32)
        for j in range(GROUP):
            block = jnp.concatenate(
                [blocks_ref[step * GROUP + j, k] for k in range(near_count)], axis=1
            )
            made = lax.dot_general(source, block, NT, preferred_element_type=jnp.float32)
            total = jnp.where(row == j, made, total)
        near_ref[place, :] = total


def far_choice(peers, admissible_ref, hot_ref):
    far_count, tile_dev = admissible_ref.shape
    tiles = peers * tile_dev
    band = tiles // far_count
    first = lax.axis_index("clus") * tile_dev
    entry = lax.broadcasted_iota(jnp.int32, (far_count, tile_dev), 0)
    place = admissible_ref[...] - first - entry * band
    place = jnp.where(place < 0, place + tiles, place)
    place = jnp.where(place < 0, place + tiles, place)
    place = jnp.concatenate([place, place], axis=1)
    owner, tile = place // tile_dev, place % tile_dev
    lane = lax.broadcasted_iota(jnp.int32, (far_count, 2 * tile_dev), 1)
    part = jnp.where(lane < tile_dev, 0, GROUP)
    line = owner * 2 * tile_dev + (tile >> 3) * 2 * GROUP + part + (tile & (GROUP - 1))
    for k in range(far_count):
        hot_ref[k] = one_hot(hot_ref.shape[1], line[k : k + 1])


def pack_coupling(coupling_ref, packed_ref):
    half = packed_ref.shape[1]

    @pl.loop(0, packed_ref.shape[0])
    def _(r):
        for k in range(half):
            pair = [coupling_ref[k, r], coupling_ref[k + half, r]]
            packed_ref[r, k] = jnp.concatenate(pair, axis=1).astype(jnp.float32)


def far_mix(peers, coeff_ref, hot_ref, packed_ref, picked_ref, mixed_ref):
    rank, half = packed_ref.shape[:2]
    far_count, span, count = hot_ref.shape
    span //= count
    stride = peers // far_count
    tile_dev = count // 2

    def found(k):
        held = jnp.concatenate(
            [coeff_ref[(k * stride + j) % peers] for j in range(span)], axis=1
        )
        return jnp.dot(held, hot_ref[k], preferred_element_type=jnp.float32)

    for k in range(half):
        both = [found(k), found(k + half)]
        for c in range(2):
            own = slice(c * tile_dev, (c + 1) * tile_dev)
            picked_ref[c, k] = jnp.concatenate([one[:, own] for one in both], axis=1)

    @pl.loop(0, rank // MIX_STEP)
    def _(step):
        total = [[0.0, 0.0] for _ in range(MIX_STEP)]
        for k in range(half):
            held = [picked_ref[c, k] for c in range(2)]
            for j in range(MIX_STEP):
                block = packed_ref[step * MIX_STEP + j, k]
                total[j] = [total[j][c] + block * held[c] for c in range(2)]
        for c in range(2):
            for j in range(MIX_STEP):
                mixed_ref[c, pl.ds(step * MIX_STEP + j, 1), :] = fold(total[j][c])


def voltages(mixed_ref, basis_ref, near_ref, flow_ref, resistance_ref, voltage_ref):
    rank, tile_dev = mixed_ref.shape[1], mixed_ref.shape[2] // 2
    width = GROUP * rank
    repeat = lax.broadcasted_iota(jnp.int32, (rank, width), 1) % rank
    repeat = jnp.where(
        lax.broadcasted_iota(jnp.int32, (rank, width), 0) == repeat, 1.0, 0.0
    ).astype(jnp.bfloat16)
    both = mixed_ref[...]
    both = both[:, :, :tile_dev] + both[:, :, tile_dev:]
    turned = jnp.concatenate([both[0], both[1]], axis=1).T.astype(jnp.bfloat16)
    wide = jnp.dot(turned, repeat, preferred_element_type=jnp.float32)
    wide = [wide[:tile_dev], wide[tile_dev:]]
    mask = lax.broadcasted_iota(jnp.int32, (GROUP, width), 1) // rank
    mask = mask == lax.broadcasted_iota(jnp.int32, (GROUP, width), 0)
    for group in range(tile_dev // GROUP):
        own = slice(group * GROUP, (group + 1) * GROUP)
        mixed = jnp.concatenate([jnp.where(mask, wide[c][own], 0.0) for c in range(2)], axis=0)
        far = jnp.dot(
            mixed.astype(jnp.bfloat16),
            basis_ref[group * width : (group + 1) * width, :],
            preferred_element_type=jnp.float32,
        )
        place = slice(group * 2 * GROUP, (group + 1) * 2 * GROUP)
        reactive = near_ref[place, :] + far
        flow = flow_ref[place, :]
        resistance = resistance_ref[own, :]
        voltage = jnp.concatenate(
            [
                resistance * flow[:GROUP] - reactive[GROUP:],
                resistance * flow[GROUP:] + reactive[:GROUP],
            ],
            axis=0,
        )
        for part, value in enumerate(halves(voltage)):
            voltage_ref[part, place, :] = value


def port_sums(current, z_ref):
    products = [
        lax.dot_general(
            current,
            z_ref[part],
            NT,
            precision=lax.Precision.HIGHEST,
            preferred_element_type=jnp.float32,
        )
        for part in range(2)
    ]
    return [products[0][0:1] - products[1][1:2], products[0][1:2] + products[1][0:1]]


def whole_kernel(
    peers,
    need_hbm,
    current_hbm,
    port_hbm,
    entry_hbm,
    sign_hbm,
    basis_in_hbm,
    source_hbm,
    blocks_hbm,
    admissible_hbm,
    coupling_hbm,
    basis_out_hbm,
    resistance_hbm,
    z_hbm,
    o_ref,
    need_ref,
    current_ref,
    port_ref,
    entry_ref,
    sign_ref,
    basis_in_ref,
    source_ref,
    blocks_ref,
    admissible_ref,
    coupling_ref,
    basis_out_ref,
    resistance_ref,
    z_ref,
    asked_ref,
    reply_ref,
    answer_ref,
    flow_ref,
    coeff_ref,
    near_hot_ref,
    near_picked_ref,
    near_ref,
    far_hot_ref,
    packed_ref,
    sum_hot_ref,
    picked_ref,
    mixed_ref,
    voltage_ref,
    slots_ref,
    arrived_ref,
    send_sem,
    recv_sem,
    load_sem,
):
    me = lax.axis_index("clus")
    met = greet(peers)
    pairs = [
        (need_hbm, need_ref),
        (current_hbm, current_ref),
        (entry_hbm, entry_ref),
        (sign_hbm, sign_ref),
        (port_hbm, port_ref),
        (source_hbm, source_ref),
        (admissible_hbm, admissible_ref),
        (basis_in_hbm, basis_in_ref),
        (blocks_hbm, blocks_ref),
        (coupling_hbm, coupling_ref),
        (basis_out_hbm, basis_out_ref),
        (resistance_hbm, resistance_ref),
        (z_hbm, z_ref),
    ]
    loads = [
        pltpu.make_async_copy(source, target, load_sem.at[i])
        for i, (source, target) in enumerate(pairs)
    ]
    for load in loads:
        load.start()
    (
        need_load,
        current_load,
        entry_load,
        sign_load,
        port_load,
        source_load,
        admissible_load,
        basis_in_load,
        blocks_load,
        coupling_load,
        basis_out_load,
        resistance_load,
        z_load,
    ) = loads
    sems = (send_sem, recv_sem)
    mesh_rows = current_ref.shape[0]
    ports = port_ref.shape[1]
    asked_ref[me] = jnp.full(asked_ref.shape[1:], -1, jnp.int32)
    need_load.wait()
    met()
    arrive, leave_need = push(
        peers,
        0,
        lambda step, peer: need_ref.at[peer],
        lambda step, own: asked_ref.at[own],
        *sems,
    )
    current_load.wait()
    entry_load.wait()
    sign_load.wait()
    own_tables = [blocks_of(current_ref[:, c, :]) for c in range(2)]
    branch_flows(own_tables, 0, False, LOCAL_CHUNK, entry_ref, sign_ref, flow_ref)
    port_load.wait()
    port = jnp.concatenate(
        [port_ref[...], jnp.full((1, LANES - ports), -1, jnp.int32)], axis=1
    ) - me * (mesh_rows * LANES)
    port_row = port >> 7
    held = pick(own_tables, port & (LANES - 1), port_row)
    port_current = [fold(held[c]) for c in range(2)]
    arrive()
    for p in range(peers):
        asked = asked_ref[p]
        found = pick(own_tables, asked & (LANES - 1), asked >> 7)
        reply_ref[p] = jnp.concatenate([fold(found[c]) for c in range(2)] + port_current, axis=0)
    arrive, leave_reply = push(
        peers,
        1,
        lambda step, peer: reply_ref.at[peer],
        lambda step, own: answer_ref.at[own],
        *sems,
    )
    answer_ref[me] = jnp.concatenate([jnp.zeros((2, LANES), jnp.float32)] + port_current, axis=0)
    source_load.wait()
    near_choice(source_ref, near_hot_ref)
    admissible_load.wait()
    far_choice(peers, admissible_ref, far_hot_ref)
    signed_hot(entry_ref, sign_ref, sum_hot_ref)
    coupling_load.wait()
    pack_coupling(coupling_ref, packed_ref)
    basis_in_load.wait()
    arrive()
    tables = [blocks_of(answer_ref[:, c, :]) for c in range(2)]
    branch_flows(tables, mesh_rows, True, REMOTE_CHUNK, entry_ref, sign_ref, flow_ref)
    far_coefficients(basis_in_ref, flow_ref, coeff_ref.at[0])
    arrive, leave_coeff = push(
        peers,
        2,
        lambda step, peer: coeff_ref.at[0],
        lambda step, own: coeff_ref.at[peers - step],
        *sems,
    )
    blocks_load.wait()
    near_work(flow_ref, near_hot_ref, blocks_ref, near_picked_ref, near_ref)
    basis_out_load.wait()
    resistance_load.wait()
    arrive()
    far_mix(peers, coeff_ref, far_hot_ref, packed_ref, picked_ref, mixed_ref)
    voltages(mixed_ref, basis_out_ref, near_ref, flow_ref, resistance_ref, voltage_ref)
    remote = collect(entry_ref, sum_hot_ref, voltage_ref, mesh_rows, peers, REMOTE_CHUNK)
    for c in range(2):
        slots_ref[:, c, :] = remote[c * peers : (c + 1) * peers, :]
    arrive, leave_slots = push(
        peers,
        3,
        lambda step, peer: slots_ref.at[peer],
        lambda step, own: arrived_ref.at[own],
        *sems,
    )
    arrived_ref[me] = jnp.zeros(arrived_ref.shape[1:], jnp.float32)
    local = collect(entry_ref, sum_hot_ref, voltage_ref, 0, mesh_rows, LOCAL_CHUNK)
    z_load.wait()
    current = answer_ref[0]
    for p in range(1, peers):
        current = current + answer_ref[p]
    port_voltage = [
        jnp.concatenate([value, jnp.zeros((1, LANES - ports), jnp.float32)], axis=1)
        for value in port_sums(current[2:4, :ports], z_ref)
    ]
    asked = jnp.concatenate([asked_ref[p] for p in range(peers)] + [port], axis=1)
    for leave in (leave_need, leave_reply, leave_coeff):
        leave()
    arrive()
    values = [
        jnp.concatenate([arrived_ref[p, c : c + 1] for p in range(peers)] + [port_voltage[c]], axis=1)
        for c in range(2)
    ]
    high, low = zip(*[halves(value) for value in values])
    spread = spread_over(high + low, asked >> 7, mesh_rows)
    total = local + join(add_up(one_hot(LANES, asked & (LANES - 1)), spread))
    for c in range(2):
        o_ref[c] = total[c * mesh_rows : (c + 1) * mesh_rows]
    leave_slots()


def per_device(
    mesh_current,
    branch_entry,
    branch_sign,
    need_slots,
    resistance,
    near_blocks,
    near_source,
    basis_in,
    coupling,
    basis_out,
    admissible,
    port_mesh,
    port_coupling,
):
    peers = lax.axis_size("clus")
    mesh_dev = mesh_current.shape[1]
    tile_dev, near_count, tile_width = near_blocks.shape[:3]
    rank = basis_in.shape[1]
    mesh_rows = mesh_dev // LANES
    far_count = admissible.shape[1]
    band = peers * tile_dev // far_count
    span = (band + tile_dev - 2) // tile_dev + 1
    operands = [
        need_slots[:, None, :],
        mesh_current.reshape(2, mesh_rows, LANES).transpose(1, 0, 2),
        port_mesh[None, :],
        branch_entry,
        branch_sign,
        basis_in.reshape(tile_dev * rank, tile_width),
        near_source.T,
        near_blocks,
        admissible.T,
        coupling.transpose(1, 2, 3, 0),
        basis_out.reshape(tile_dev * rank, tile_width),
        resistance.reshape(tile_dev, tile_width),
        port_coupling,
    ]
    f32, bf16 = jnp.float32, jnp.bfloat16
    tiles = pltpu.VMEM((2 * tile_dev, LANES), f32)
    message = pltpu.VMEM((peers, 2, LANES), f32)
    made = pl.pallas_call(
        functools.partial(whole_kernel, peers),
        out_shape=jax.ShapeDtypeStruct((2, mesh_rows, LANES), f32),
        in_specs=[pl.BlockSpec(memory_space=pltpu.HBM)] * len(operands),
        out_specs=pl.BlockSpec(memory_space=pltpu.VMEM),
        scratch_shapes=[pltpu.VMEM(x.shape, x.dtype) for x in operands]
        + [
            pltpu.VMEM((peers, 1, LANES), jnp.int32),
            pltpu.VMEM((peers, 4, LANES), f32),
            pltpu.VMEM((peers, 4, LANES), f32),
            tiles,
            pltpu.VMEM((peers, rank, 2 * tile_dev), bf16),
            pltpu.VMEM((near_count, 2 * tile_dev, 2 * tile_dev), bf16),
            pltpu.VMEM((2 * tile_dev, near_count * LANES), bf16),
            tiles,
            pltpu.VMEM((far_count, span * 2 * tile_dev, 2 * tile_dev), bf16),
            pltpu.VMEM((rank, far_count // 2, rank, 2 * tile_dev), f32),
            pltpu.VMEM((branch_entry.shape[0], LANES, branch_entry.shape[1]), bf16),
            pltpu.VMEM((2, far_count // 2, rank, 2 * tile_dev), f32),
            pltpu.VMEM((2, rank, 2 * tile_dev), f32),
            pltpu.VMEM((2, 2 * tile_dev, LANES), f32),
            message,
            message,
            pltpu.SemaphoreType.DMA((4, peers)),
            pltpu.SemaphoreType.DMA((4, peers)),
            pltpu.SemaphoreType.DMA((len(operands),)),
        ],
        compiler_params=pltpu.CompilerParams(
            collective_id=0, has_side_effects=True, vmem_limit_bytes=VMEM_LIMIT
        ),
    )(*operands)
    return made.reshape(2, mesh_dev)


def solution(mesh):
    both = ("groups", "clus")
    in_specs = (
        P(None, both),
        P(None, both),
        P(None, both),
        P(both, None),
        P(both),
        P(both, None, None, None),
        P(both, None),
        P(both, None, None),
        P(both, None, None, None),
        P(both, None, None),
        P(both, None),
        P("groups"),
        P(),
    )
    return jax.shard_map(
        per_device, mesh=mesh, in_specs=in_specs, out_specs=P(None, both), check_vma=False
    )
```

```python
import functools

import jax
import jax.numpy as jnp
from jax import lax
from jax.experimental import pallas as pl
from jax.experimental.pallas import tpu as pltpu
from jax.sharding import PartitionSpec as P

LANES = 128
GROUP = 8
LOCAL_CHUNK = 2048
REMOTE_CHUNK = 8192
HOT_CHUNK = 1024
MIX_STEP = 4
VMEM_LIMIT = 44 * 1024 * 1024
NT = (((1,), (1,)), ((), ()))


def greet(peers):
    me = lax.axis_index("clus")
    barrier = pltpu.get_barrier_semaphore()
    for step in range(1, peers):
        pl.semaphore_signal(
            barrier,
            inc=1,
            device_id={"clus": lax.rem(me + step, peers)},
            device_id_type=pl.DeviceIdType.MESH,
        )
    return lambda: pl.semaphore_wait(barrier, peers - 1)


def partner(peers, step):
    me = lax.axis_index("clus")
    if peers & (peers - 1):
        return lax.rem(me + step, peers)
    peer, bit = me, 1
    while bit < peers:
        if step & bit:
            peer = peer + bit * (1 - 2 * lax.rem(lax.div(me, bit), 2))
        bit *= 2
    return peer


def push(peers, phase, source_at, target_at, send_sem, recv_sem):
    me = lax.axis_index("clus")
    copies = []
    for step in range(peers - 1, 0, -1):
        peer = partner(peers, step)
        copy = pltpu.make_async_remote_copy(
            src_ref=source_at(peer),
            dst_ref=target_at(peer, me),
            send_sem=send_sem.at[phase, step],
            recv_sem=recv_sem.at[phase, step],
            device_id={"clus": peer},
            device_id_type=pl.DeviceIdType.MESH,
        )
        copy.start()
        copies.append(copy)

    def arrive():
        for copy in copies:
            copy.wait_recv()

    def leave():
        for copy in copies:
            copy.wait_send()

    return arrive, leave


def one_hot(rows, index):
    match = lax.broadcasted_iota(jnp.int32, (rows, index.shape[1]), 0) == index
    return jnp.where(match, 1.0, 0.0).astype(jnp.bfloat16)


def pick(tables, low, row):
    sub = lax.broadcasted_iota(jnp.int32, (GROUP, LANES), 0)
    lanes = jnp.broadcast_to(low, (GROUP, LANES))
    gap = jnp.broadcast_to(row, (GROUP, LANES)) - sub
    total = [0.0, 0.0]
    for block in range(len(tables[0])):
        match = gap == block * GROUP
        for c in range(2):
            found = jnp.take_along_axis(
                tables[c][block], lanes, axis=1, mode="promise_in_bounds"
            )
            total[c] += jnp.where(match, found, 0.0)
    return total


def fold(value):
    return jnp.sum(value, axis=0, keepdims=True)


def blocks_of(table):
    return [table[start : start + GROUP] for start in range(0, table.shape[0], GROUP)]


def branch_flows(tables, first_row, add, chunk, entry_ref, sign_ref, flow_ref):
    chunk = min(chunk, entry_ref.shape[1])
    groups = chunk // (GROUP * LANES)

    @pl.loop(0, entry_ref.shape[1] // chunk)
    def _(step):
        for group in range(groups):
            rows = [[], []]
            for j in range(GROUP):
                start = step * chunk + (group * GROUP + j) * LANES
                columns = pl.ds(pl.multiple_of(start, LANES), LANES)
                total = [0.0, 0.0]
                for k in range(entry_ref.shape[0]):
                    entry = entry_ref[k : k + 1, columns]
                    orient = (2 * sign_ref[k : k + 1, columns] - 1).astype(jnp.float32)
                    found = pick(tables, entry & (LANES - 1), (entry >> 7) - first_row)
                    total = [total[c] + orient * found[c] for c in range(2)]
                for c in range(2):
                    rows[c].append(fold(total[c]))
            for c in range(2):
                start = (step * groups + group) * 2 * GROUP + c * GROUP
                place = pl.ds(pl.multiple_of(start, GROUP), GROUP)
                made = jnp.concatenate(rows[c], axis=0)
                flow_ref[place, :] = flow_ref[place, :] + made if add else made


def signed_hot(entry_ref, sign_ref, hot_ref):
    @pl.loop(0, entry_ref.shape[1] // HOT_CHUNK)
    def _(step):
        columns = pl.ds(pl.multiple_of(step * HOT_CHUNK, HOT_CHUNK), HOT_CHUNK)
        for k in range(entry_ref.shape[0]):
            orient = (2 * sign_ref[k : k + 1, columns] - 1).astype(jnp.float32)
            low = entry_ref[k : k + 1, columns] & (LANES - 1)
            match = lax.broadcasted_iota(jnp.int32, (LANES, HOT_CHUNK), 0) == low
            hot_ref[k, :, columns] = jnp.where(match, orient, 0.0).astype(jnp.bfloat16)


def halves(value):
    high = value.astype(jnp.bfloat16).astype(jnp.float32)
    return high, value - high


def spread_over(parts, row, rows):
    mask = lax.broadcasted_iota(jnp.int32, (rows, row.shape[1]), 0) == row
    return jnp.concatenate(
        [jnp.where(mask, part, 0.0).astype(jnp.bfloat16) for part in parts], axis=0
    )


def add_up(hot, spread):
    return lax.dot_general(hot, spread, NT, preferred_element_type=jnp.float32)


def join(made):
    turned = made.T
    half = turned.shape[0] // 2
    return turned[:half] + turned[half:]


def collect(entry_ref, hot_ref, voltage_ref, first_row, rows, chunk):
    count = entry_ref.shape[1]
    chunk = min(chunk, count)
    groups = chunk // (GROUP * LANES)

    def body(step, total):
        columns = pl.ds(pl.multiple_of(step * chunk, chunk), chunk)
        parts = []
        for part in range(2):
            for c in range(2):
                lines = []
                for group in range(groups):
                    start = (step * groups + group) * 2 * GROUP + c * GROUP
                    tile = voltage_ref[part, pl.ds(pl.multiple_of(start, GROUP), GROUP), :]
                    lines += [tile[j : j + 1] for j in range(GROUP)]
                parts.append(jnp.concatenate(lines, axis=1))
        for k in range(entry_ref.shape[0]):
            row = (entry_ref[k : k + 1, columns] >> 7) - first_row
            total += add_up(hot_ref[k, :, columns], spread_over(parts, row, rows))
        return total

    total = jnp.zeros((LANES, 4 * rows), jnp.float32)
    if count == chunk:
        return join(body(0, total))
    return join(lax.fori_loop(0, count // chunk, body, total))


def far_coefficients(basis_ref, flow_ref, o_ref):
    flows = flow_ref[...].astype(jnp.bfloat16)
    count = flows.shape[0]
    tile_dev = count // 2
    rank = basis_ref.shape[0] // tile_dev
    lane = lax.broadcasted_iota(jnp.int32, (rank, count), 1)
    tile = (lane >> 4) * GROUP + (lane & (GROUP - 1))
    total = jnp.zeros((rank, count), jnp.float32)
    for start in range(0, tile_dev, GROUP):
        crossed = lax.dot_general(
            basis_ref[start * rank : (start + GROUP) * rank, :],
            flows,
            NT,
            preferred_element_type=jnp.float32,
        )
        for j in range(GROUP):
            total = jnp.where(tile == start + j, crossed[j * rank : (j + 1) * rank], total)
    o_ref[...] = total.astype(jnp.bfloat16)


def near_choice(source_ref, hot_ref):
    near_count, tile_dev = source_ref.shape
    count = 2 * tile_dev
    lane = lax.broadcasted_iota(jnp.int32, (tile_dev, count), 1)
    tile = (lane >> 4) * GROUP + (lane & (GROUP - 1))
    widen = lax.broadcasted_iota(jnp.int32, (tile_dev, count), 0) == tile
    source = jnp.dot(
        source_ref[...].astype(jnp.float32).astype(jnp.bfloat16),
        jnp.where(widen, 1.0, 0.0).astype(jnp.bfloat16),
        preferred_element_type=jnp.float32,
    ).astype(jnp.int32)
    part = lax.broadcasted_iota(jnp.int32, (near_count, count), 1) & GROUP
    place = (source >> 3) * 2 * GROUP + part + (source & (GROUP - 1))
    for k in range(near_count):
        hot = jnp.where(
            lax.broadcasted_iota(jnp.int32, (count, count), 0) == place[k : k + 1], 1.0, 0.0
        )
        hot_ref[k] = hot.T.astype(jnp.bfloat16)


def near_work(flow_ref, hot_ref, blocks_ref, picked_ref, near_ref):
    near_count = blocks_ref.shape[1]
    flows = flow_ref[...].astype(jnp.bfloat16)
    for k in range(near_count):
        picked_ref[:, k * LANES : (k + 1) * LANES] = jnp.dot(
            hot_ref[k], flows, preferred_element_type=jnp.float32
        ).astype(jnp.bfloat16)

    @pl.loop(0, blocks_ref.shape[0] // GROUP)
    def _(step):
        place = pl.ds(pl.multiple_of(step * 2 * GROUP, 2 * GROUP), 2 * GROUP)
        source = picked_ref[place, :]
        row = lax.broadcasted_iota(jnp.int32, (2 * GROUP, LANES), 0) & (GROUP - 1)
        total = jnp.zeros((2 * GROUP, LANES), jnp.float32)
        for j in range(GROUP):
            block = jnp.concatenate(
                [blocks_ref[step * GROUP + j, k] for k in range(near_count)], axis=1
            )
            made = lax.dot_general(source, block, NT, preferred_element_type=jnp.float32)
            total = jnp.where(row == j, made, total)
        near_ref[place, :] = total


def far_choice(peers, admissible_ref, hot_ref):
    far_count, tile_dev = admissible_ref.shape
    tiles = peers * tile_dev
    band = tiles // far_count
    first = lax.axis_index("clus") * tile_dev
    entry = lax.broadcasted_iota(jnp.int32, (far_count, tile_dev), 0)
    place = admissible_ref[...] - first - entry * band
    place = jnp.where(place < 0, place + tiles, place)
    place = jnp.where(place < 0, place + tiles, place)
    place = jnp.concatenate([place, place], axis=1)
    owner, tile = place // tile_dev, place % tile_dev
    lane = lax.broadcasted_iota(jnp.int32, (far_count, 2 * tile_dev), 1)
    part = jnp.where(lane < tile_dev, 0, GROUP)
    line = owner * 2 * tile_dev + (tile >> 3) * 2 * GROUP + part + (tile & (GROUP - 1))
    for k in range(far_count):
        hot_ref[k] = one_hot(hot_ref.shape[1], line[k : k + 1])


def pack_coupling(coupling_ref, packed_ref):
    half = packed_ref.shape[1]

    @pl.loop(0, packed_ref.shape[0])
    def _(r):
        for k in range(half):
            pair = [coupling_ref[k, r], coupling_ref[k + half, r]]
            packed_ref[r, k] = jnp.concatenate(pair, axis=1).astype(jnp.float32)


def far_mix(peers, coeff_ref, hot_ref, packed_ref, picked_ref, partial_ref, mixed_ref):
    rank, half = packed_ref.shape[:2]
    far_count, span, count = hot_ref.shape
    span //= count
    stride = peers // far_count
    tile_dev = count // 2

    def found(k):
        held = jnp.concatenate(
            [coeff_ref[(k * stride + j) % peers] for j in range(span)], axis=1
        )
        return jnp.dot(held, hot_ref[k], preferred_element_type=jnp.float32)

    for k in range(half):
        both = [found(k), found(k + half)]
        for c in range(2):
            own = slice(c * tile_dev, (c + 1) * tile_dev)
            picked_ref[c, k] = jnp.concatenate([one[:, own] for one in both], axis=1)

    @pl.loop(0, rank // MIX_STEP)
    def _(step):
        total = [[0.0, 0.0] for _ in range(MIX_STEP)]
        for k in range(half):
            held = [picked_ref[c, k] for c in range(2)]
            for j in range(MIX_STEP):
                block = packed_ref[step * MIX_STEP + j, k]
                total[j] = [total[j][c] + block * held[c] for c in range(2)]
        for c in range(2):
            for j in range(MIX_STEP):
                blocks = blocks_of(total[j][c])
                partial_ref[c, step * MIX_STEP + j] = functools.reduce(jnp.add, blocks)

    for c in range(2):
        for start in range(0, rank, GROUP):
            mixed_ref[c, start : start + GROUP, :] = jnp.concatenate(
                [fold(partial_ref[c, start + j]) for j in range(GROUP)], axis=0
            )


def voltages(mixed_ref, basis_ref, near_ref, flow_ref, resistance_ref, voltage_ref):
    rank, tile_dev = mixed_ref.shape[1], mixed_ref.shape[2] // 2
    width = GROUP * rank
    repeat = lax.broadcasted_iota(jnp.int32, (rank, width), 1) % rank
    repeat = jnp.where(
        lax.broadcasted_iota(jnp.int32, (rank, width), 0) == repeat, 1.0, 0.0
    ).astype(jnp.bfloat16)
    both = mixed_ref[...]
    both = both[:, :, :tile_dev] + both[:, :, tile_dev:]
    turned = jnp.concatenate([both[0], both[1]], axis=1).T.astype(jnp.bfloat16)
    wide = jnp.dot(turned, repeat, preferred_element_type=jnp.float32)
    wide = [wide[:tile_dev], wide[tile_dev:]]
    mask = lax.broadcasted_iota(jnp.int32, (GROUP, width), 1) // rank
    mask = mask == lax.broadcasted_iota(jnp.int32, (GROUP, width), 0)
    for group in range(tile_dev // GROUP):
        own = slice(group * GROUP, (group + 1) * GROUP)
        mixed = jnp.concatenate([jnp.where(mask, wide[c][own], 0.0) for c in range(2)], axis=0)
        far = jnp.dot(
            mixed.astype(jnp.bfloat16),
            basis_ref[group * width : (group + 1) * width, :],
            preferred_element_type=jnp.float32,
        )
        place = slice(group * 2 * GROUP, (group + 1) * 2 * GROUP)
        reactive = near_ref[place, :] + far
        flow = flow_ref[place, :]
        resistance = resistance_ref[own, :]
        voltage = jnp.concatenate(
            [
                resistance * flow[:GROUP] - reactive[GROUP:],
                resistance * flow[GROUP:] + reactive[:GROUP],
            ],
            axis=0,
        )
        for part, value in enumerate(halves(voltage)):
            voltage_ref[part, place, :] = value


def port_sums(current, z_ref):
    products = [
        lax.dot_general(
            current,
            z_ref[part],
            NT,
            precision=lax.Precision.HIGHEST,
            preferred_element_type=jnp.float32,
        )
        for part in range(2)
    ]
    return [products[0][0:1] - products[1][1:2], products[0][1:2] + products[1][0:1]]


def whole_kernel(
    peers,
    need_hbm,
    current_hbm,
    port_hbm,
    entry_hbm,
    sign_hbm,
    basis_in_hbm,
    source_hbm,
    blocks_hbm,
    admissible_hbm,
    coupling_hbm,
    basis_out_hbm,
    resistance_hbm,
    z_hbm,
    o_ref,
    need_ref,
    current_ref,
    port_ref,
    entry_ref,
    sign_ref,
    basis_in_ref,
    source_ref,
    blocks_ref,
    admissible_ref,
    coupling_ref,
    basis_out_ref,
    resistance_ref,
    z_ref,
    asked_ref,
    reply_ref,
    answer_ref,
    flow_ref,
    coeff_ref,
    near_hot_ref,
    near_picked_ref,
    near_ref,
    far_hot_ref,
    packed_ref,
    sum_hot_ref,
    picked_ref,
    partial_ref,
    mixed_ref,
    voltage_ref,
    slots_ref,
    arrived_ref,
    send_sem,
    recv_sem,
    load_sem,
):
    me = lax.axis_index("clus")
    met = greet(peers)
    pairs = [
        (need_hbm, need_ref),
        (current_hbm, current_ref),
        (entry_hbm, entry_ref),
        (sign_hbm, sign_ref),
        (port_hbm, port_ref),
        (source_hbm, source_ref),
        (admissible_hbm, admissible_ref),
        (basis_in_hbm, basis_in_ref),
        (blocks_hbm, blocks_ref),
        (coupling_hbm, coupling_ref),
        (basis_out_hbm, basis_out_ref),
        (resistance_hbm, resistance_ref),
        (z_hbm, z_ref),
    ]
    loads = [
        pltpu.make_async_copy(source, target, load_sem.at[i])
        for i, (source, target) in enumerate(pairs)
    ]
    for load in loads:
        load.start()
    (
        need_load,
        current_load,
        entry_load,
        sign_load,
        port_load,
        source_load,
        admissible_load,
        basis_in_load,
        blocks_load,
        coupling_load,
        basis_out_load,
        resistance_load,
        z_load,
    ) = loads
    sems = (send_sem, recv_sem)
    mesh_rows = current_ref.shape[0]
    ports = port_ref.shape[1]
    asked_ref[me] = jnp.full(asked_ref.shape[1:], -1, jnp.int32)
    need_load.wait()
    met()
    arrive, leave_need = push(
        peers,
        0,
        lambda peer: need_ref.at[peer],
        lambda peer, own: asked_ref.at[own],
        *sems,
    )
    current_load.wait()
    entry_load.wait()
    sign_load.wait()
    own_tables = [blocks_of(current_ref[:, c, :]) for c in range(2)]
    branch_flows(own_tables, 0, False, LOCAL_CHUNK, entry_ref, sign_ref, flow_ref)
    port_load.wait()
    port = jnp.concatenate(
        [port_ref[...], jnp.full((1, LANES - ports), -1, jnp.int32)], axis=1
    ) - me * (mesh_rows * LANES)
    port_row = port >> 7
    held = pick(own_tables, port & (LANES - 1), port_row)
    port_current = [fold(held[c]) for c in range(2)]
    arrive()
    for p in range(peers):
        asked = asked_ref[p]
        found = pick(own_tables, asked & (LANES - 1), asked >> 7)
        reply_ref[p] = jnp.concatenate([fold(found[c]) for c in range(2)] + port_current, axis=0)
    arrive, leave_reply = push(
        peers,
        1,
        lambda peer: reply_ref.at[peer],
        lambda peer, own: answer_ref.at[own],
        *sems,
    )
    answer_ref[me] = jnp.concatenate([jnp.zeros((2, LANES), jnp.float32)] + port_current, axis=0)
    source_load.wait()
    near_choice(source_ref, near_hot_ref)
    admissible_load.wait()
    far_choice(peers, admissible_ref, far_hot_ref)
    signed_hot(entry_ref, sign_ref, sum_hot_ref)
    coupling_load.wait()
    pack_coupling(coupling_ref, packed_ref)
    basis_in_load.wait()
    arrive()
    tables = [blocks_of(answer_ref[:, c, :]) for c in range(2)]
    branch_flows(tables, mesh_rows, True, REMOTE_CHUNK, entry_ref, sign_ref, flow_ref)
    far_coefficients(basis_in_ref, flow_ref, coeff_ref.at[0])
    arrive, leave_coeff = push(
        peers,
        2,
        lambda peer: coeff_ref.at[0],
        lambda peer, own: coeff_ref.at[lax.rem(own - peer + peers, peers)],
        *sems,
    )
    blocks_load.wait()
    near_work(flow_ref, near_hot_ref, blocks_ref, near_picked_ref, near_ref)
    basis_out_load.wait()
    resistance_load.wait()
    arrive()
    far_mix(peers, coeff_ref, far_hot_ref, packed_ref, picked_ref, partial_ref, mixed_ref)
    voltages(mixed_ref, basis_out_ref, near_ref, flow_ref, resistance_ref, voltage_ref)
    remote = collect(entry_ref, sum_hot_ref, voltage_ref, mesh_rows, peers, REMOTE_CHUNK)
    for c in range(2):
        slots_ref[:, c, :] = remote[c * peers : (c + 1) * peers, :]
    arrive, leave_slots = push(
        peers,
        3,
        lambda peer: slots_ref.at[peer],
        lambda peer, own: arrived_ref.at[own],
        *sems,
    )
    arrived_ref[me] = jnp.zeros(arrived_ref.shape[1:], jnp.float32)
    local = collect(entry_ref, sum_hot_ref, voltage_ref, 0, mesh_rows, LOCAL_CHUNK)
    z_load.wait()
    current = answer_ref[0]
    for p in range(1, peers):
        current = current + answer_ref[p]
    port_voltage = [
        jnp.concatenate([value, jnp.zeros((1, LANES - ports), jnp.float32)], axis=1)
        for value in port_sums(current[2:4, :ports], z_ref)
    ]
    asked = jnp.concatenate([asked_ref[p] for p in range(peers)] + [port], axis=1)
    asked_hot = one_hot(LANES, asked & (LANES - 1))
    for leave in (leave_need, leave_reply, leave_coeff):
        leave()
    arrive()
    values = [
        jnp.concatenate([arrived_ref[p, c : c + 1] for p in range(peers)] + [port_voltage[c]], axis=1)
        for c in range(2)
    ]
    high, low = zip(*[halves(value) for value in values])
    spread = spread_over(high + low, asked >> 7, mesh_rows)
    made = add_up(spread, asked_hot)
    total = local + made[: 2 * mesh_rows] + made[2 * mesh_rows :]
    for c in range(2):
        o_ref[c] = total[c * mesh_rows : (c + 1) * mesh_rows]
    leave_slots()


def per_device(
    mesh_current,
    branch_entry,
    branch_sign,
    need_slots,
    resistance,
    near_blocks,
    near_source,
    basis_in,
    coupling,
    basis_out,
    admissible,
    port_mesh,
    port_coupling,
):
    peers = lax.axis_size("clus")
    mesh_dev = mesh_current.shape[1]
    tile_dev, near_count, tile_width = near_blocks.shape[:3]
    rank = basis_in.shape[1]
    mesh_rows = mesh_dev // LANES
    far_count = admissible.shape[1]
    band = peers * tile_dev // far_count
    span = (band + tile_dev - 2) // tile_dev + 1
    operands = [
        need_slots[:, None, :],
        mesh_current.reshape(2, mesh_rows, LANES).transpose(1, 0, 2),
        port_mesh[None, :],
        branch_entry,
        branch_sign,
        basis_in.reshape(tile_dev * rank, tile_width),
        near_source.T,
        near_blocks,
        admissible.T,
        coupling.transpose(1, 2, 3, 0),
        basis_out.reshape(tile_dev * rank, tile_width),
        resistance.reshape(tile_dev, tile_width),
        port_coupling,
    ]
    f32, bf16 = jnp.float32, jnp.bfloat16
    operands = [pltpu.with_memory_space_constraint(x, pltpu.HBM) for x in operands]
    tiles = pltpu.VMEM((2 * tile_dev, LANES), f32)
    message = pltpu.VMEM((peers, 2, LANES), f32)
    made = pl.pallas_call(
        functools.partial(whole_kernel, peers),
        out_shape=jax.ShapeDtypeStruct((2, mesh_rows, LANES), f32),
        in_specs=[pl.BlockSpec(memory_space=pltpu.HBM)] * len(operands),
        out_specs=pl.BlockSpec(memory_space=pltpu.VMEM),
        scratch_shapes=[pltpu.VMEM(x.shape, x.dtype) for x in operands]
        + [
            pltpu.VMEM((peers, 1, LANES), jnp.int32),
            pltpu.VMEM((peers, 4, LANES), f32),
            pltpu.VMEM((peers, 4, LANES), f32),
            tiles,
            pltpu.VMEM((peers, rank, 2 * tile_dev), bf16),
            pltpu.VMEM((near_count, 2 * tile_dev, 2 * tile_dev), bf16),
            pltpu.VMEM((2 * tile_dev, near_count * LANES), bf16),
            tiles,
            pltpu.VMEM((far_count, span * 2 * tile_dev, 2 * tile_dev), bf16),
            pltpu.VMEM((rank, far_count // 2, rank, 2 * tile_dev), f32),
            pltpu.VMEM((branch_entry.shape[0], LANES, branch_entry.shape[1]), bf16),
            pltpu.VMEM((2, far_count // 2, rank, 2 * tile_dev), f32),
            pltpu.VMEM((2, rank, GROUP, 2 * tile_dev), f32),
            pltpu.VMEM((2, rank, 2 * tile_dev), f32),
            pltpu.VMEM((2, 2 * tile_dev, LANES), f32),
            message,
            message,
            pltpu.SemaphoreType.DMA((4, peers)),
            pltpu.SemaphoreType.DMA((4, peers)),
            pltpu.SemaphoreType.DMA((len(operands),)),
        ],
        compiler_params=pltpu.CompilerParams(
            collective_id=0, has_side_effects=True, vmem_limit_bytes=VMEM_LIMIT
        ),
    )(*operands)
    return made.reshape(2, mesh_dev)


def solution(mesh):
    both = ("groups", "clus")
    in_specs = (
        P(None, both),
        P(None, both),
        P(None, both),
        P(both, None),
        P(both),
        P(both, None, None, None),
        P(both, None),
        P(both, None, None),
        P(both, None, None, None),
        P(both, None, None),
        P(both, None),
        P("groups"),
        P(),
    )
    return jax.shard_map(
        per_device, mesh=mesh, in_specs=in_specs, out_specs=P(None, both), check_vma=False
    )
```

```python
import functools

import jax
import jax.numpy as jnp
from jax import lax
from jax.experimental import pallas as pl
from jax.experimental.pallas import tpu as pltpu
from jax.sharding import PartitionSpec as P

LANES = 128
GROUP = 8
LOCAL_CHUNK = 2048
REMOTE_CHUNK = 8192
HOT_CHUNK = 1024
MIX_STEP = 4
VMEM_LIMIT = 44 * 1024 * 1024
NT = (((1,), (1,)), ((), ()))


def greet(peers):
    me = lax.axis_index("clus")
    barrier = pltpu.get_barrier_semaphore()
    for step in range(1, peers):
        pl.semaphore_signal(
            barrier,
            inc=1,
            device_id={"clus": lax.rem(me + step, peers)},
            device_id_type=pl.DeviceIdType.MESH,
        )
    return lambda: pl.semaphore_wait(barrier, peers - 1)


def partner(peers, step):
    me = lax.axis_index("clus")
    peer, bit = me, 1
    while bit < peers:
        if step & bit:
            peer = peer + bit * (1 - 2 * lax.rem(lax.div(me, bit), 2))
        bit *= 2
    return peer


def push(peers, phase, steps, source_at, target_at, send_sem, recv_sem):
    me = lax.axis_index("clus")
    copies = []
    for step in reversed(steps):
        peer = partner(peers, step)
        copy = pltpu.make_async_remote_copy(
            src_ref=source_at(peer),
            dst_ref=target_at(peer, me),
            send_sem=send_sem.at[phase, step],
            recv_sem=recv_sem.at[phase, step],
            device_id={"clus": peer},
            device_id_type=pl.DeviceIdType.MESH,
        )
        copy.start()
        copies.append(copy)

    def arrive():
        for copy in copies:
            copy.wait_recv()

    def leave():
        for copy in copies:
            copy.wait_send()

    return arrive, leave


def one_hot(rows, index):
    match = lax.broadcasted_iota(jnp.int32, (rows, index.shape[1]), 0) == index
    return jnp.where(match, 1.0, 0.0).astype(jnp.bfloat16)


def pick(tables, low, row):
    sub = lax.broadcasted_iota(jnp.int32, (GROUP, LANES), 0)
    lanes = jnp.broadcast_to(low, (GROUP, LANES))
    gap = jnp.broadcast_to(row, (GROUP, LANES)) - sub
    total = [0.0, 0.0]
    for block in range(len(tables[0])):
        match = gap == block * GROUP
        for c in range(2):
            found = jnp.take_along_axis(
                tables[c][block], lanes, axis=1, mode="promise_in_bounds"
            )
            total[c] += jnp.where(match, found, 0.0)
    return total


def fold(value):
    return jnp.sum(value, axis=0, keepdims=True)


def fold_rows(values):
    line = lax.broadcasted_iota(jnp.int32, (GROUP, LANES), 0)
    gap = GROUP // 2
    while gap:
        low = (line & gap) == 0

        def swap(value):
            down = pltpu.roll(value, gap, 0)
            if 2 * gap == GROUP:
                return down
            return jnp.where(low, pltpu.roll(value, GROUP - gap, 0), down)

        half = len(values) // 2
        values = [
            jnp.where(low, one, two) + swap(jnp.where(low, two, one))
            for one, two in zip(values[:half], values[half:])
        ]
        gap //= 2
    return values[0]


def blocks_of(table):
    return [table[start : start + GROUP] for start in range(0, table.shape[0], GROUP)]


def branch_flows(tables, first_row, add, chunk, entry_ref, sign_ref, flow_ref):
    chunk = min(chunk, entry_ref.shape[1])
    groups = chunk // (GROUP * LANES)

    @pl.loop(0, entry_ref.shape[1] // chunk)
    def _(step):
        for group in range(groups):
            rows = [[], []]
            for j in range(GROUP):
                start = step * chunk + (group * GROUP + j) * LANES
                columns = pl.ds(pl.multiple_of(start, LANES), LANES)
                total = [0.0, 0.0]
                for k in range(entry_ref.shape[0]):
                    entry = entry_ref[k : k + 1, columns]
                    orient = (2 * sign_ref[k : k + 1, columns] - 1).astype(jnp.float32)
                    found = pick(tables, entry & (LANES - 1), (entry >> 7) - first_row)
                    total = [total[c] + orient * found[c] for c in range(2)]
                for c in range(2):
                    rows[c].append(total[c])
            for c in range(2):
                start = (step * groups + group) * 2 * GROUP + c * GROUP
                place = pl.ds(pl.multiple_of(start, GROUP), GROUP)
                made = fold_rows(rows[c])
                flow_ref[place, :] = flow_ref[place, :] + made if add else made


def signed_hot(entry_ref, sign_ref, hot_ref):
    @pl.loop(0, entry_ref.shape[1] // HOT_CHUNK)
    def _(step):
        columns = pl.ds(pl.multiple_of(step * HOT_CHUNK, HOT_CHUNK), HOT_CHUNK)
        for k in range(entry_ref.shape[0]):
            orient = (2 * sign_ref[k : k + 1, columns] - 1).astype(jnp.float32)
            low = entry_ref[k : k + 1, columns] & (LANES - 1)
            match = lax.broadcasted_iota(jnp.int32, (LANES, HOT_CHUNK), 0) == low
            hot_ref[k, :, columns] = jnp.where(match, orient, 0.0).astype(jnp.bfloat16)


def halves(value):
    high = value.astype(jnp.bfloat16).astype(jnp.float32)
    return high, value - high


def spread_over(parts, row, rows):
    mask = lax.broadcasted_iota(jnp.int32, (rows, row.shape[1]), 0) == row
    return jnp.concatenate(
        [jnp.where(mask, part, 0.0).astype(jnp.bfloat16) for part in parts], axis=0
    )


def add_up(hot, spread):
    return lax.dot_general(hot, spread, NT, preferred_element_type=jnp.float32)


def join(made):
    turned = made.T
    half = turned.shape[0] // 2
    return turned[:half] + turned[half:]


def collect(entry_ref, hot_ref, voltage_ref, first_row, rows, chunk):
    count = entry_ref.shape[1]
    chunk = min(chunk, count)
    groups = chunk // (GROUP * LANES)

    def body(step, total):
        columns = pl.ds(pl.multiple_of(step * chunk, chunk), chunk)
        parts = []
        for part in range(2):
            for c in range(2):
                lines = []
                for group in range(groups):
                    start = (step * groups + group) * 2 * GROUP + c * GROUP
                    tile = voltage_ref[part, pl.ds(pl.multiple_of(start, GROUP), GROUP), :]
                    lines += [tile[j : j + 1] for j in range(GROUP)]
                parts.append(jnp.concatenate(lines, axis=1))
        for k in range(entry_ref.shape[0]):
            row = (entry_ref[k : k + 1, columns] >> 7) - first_row
            total += add_up(hot_ref[k, :, columns], spread_over(parts, row, rows))
        return total

    total = jnp.zeros((LANES, 4 * rows), jnp.float32)
    if count == chunk:
        return join(body(0, total))
    return join(lax.fori_loop(0, count // chunk, body, total))


def far_coefficients(basis_ref, flow_ref, o_ref):
    flows = flow_ref[...].astype(jnp.bfloat16)
    count = flows.shape[0]
    tile_dev = count // 2
    rank = basis_ref.shape[0] // tile_dev
    lane = lax.broadcasted_iota(jnp.int32, (rank, count), 1)
    tile = (lane >> 4) * GROUP + (lane & (GROUP - 1))
    total = jnp.zeros((rank, count), jnp.float32)
    for start in range(0, tile_dev, GROUP):
        crossed = lax.dot_general(
            basis_ref[start * rank : (start + GROUP) * rank, :],
            flows,
            NT,
            preferred_element_type=jnp.float32,
        )
        for j in range(GROUP):
            total = jnp.where(tile == start + j, crossed[j * rank : (j + 1) * rank], total)
    o_ref[...] = total.astype(jnp.bfloat16)


def near_choice(source_ref, hot_ref):
    near_count, tile_dev = source_ref.shape
    count = 2 * tile_dev
    lane = lax.broadcasted_iota(jnp.int32, (tile_dev, count), 1)
    tile = (lane >> 4) * GROUP + (lane & (GROUP - 1))
    widen = lax.broadcasted_iota(jnp.int32, (tile_dev, count), 0) == tile
    source = jnp.dot(
        source_ref[...].astype(jnp.float32).astype(jnp.bfloat16),
        jnp.where(widen, 1.0, 0.0).astype(jnp.bfloat16),
        preferred_element_type=jnp.float32,
    ).astype(jnp.int32)
    part = lax.broadcasted_iota(jnp.int32, (near_count, count), 1) & GROUP
    place = (source >> 3) * 2 * GROUP + part + (source & (GROUP - 1))
    for k in range(near_count):
        hot = jnp.where(
            lax.broadcasted_iota(jnp.int32, (count, count), 0) == place[k : k + 1], 1.0, 0.0
        )
        hot_ref[k] = hot.T.astype(jnp.bfloat16)


def near_work(flow_ref, hot_ref, blocks_ref, picked_ref, near_ref):
    near_count = blocks_ref.shape[1]
    flows = flow_ref[...].astype(jnp.bfloat16)
    for k in range(near_count):
        picked_ref[:, k * LANES : (k + 1) * LANES] = jnp.dot(
            hot_ref[k], flows, preferred_element_type=jnp.float32
        ).astype(jnp.bfloat16)

    @pl.loop(0, blocks_ref.shape[0] // GROUP)
    def _(step):
        place = pl.ds(pl.multiple_of(step * 2 * GROUP, 2 * GROUP), 2 * GROUP)
        source = picked_ref[place, :]
        row = lax.broadcasted_iota(jnp.int32, (2 * GROUP, LANES), 0) & (GROUP - 1)
        total = jnp.zeros((2 * GROUP, LANES), jnp.float32)
        for j in range(GROUP):
            block = jnp.concatenate(
                [blocks_ref[step * GROUP + j, k] for k in range(near_count)], axis=1
            )
            made = lax.dot_general(source, block, NT, preferred_element_type=jnp.float32)
            total = jnp.where(row == j, made, total)
        near_ref[place, :] = total


def far_choice(peers, admissible_ref, hot_ref):
    far_count, tile_dev = admissible_ref.shape
    tiles = peers * tile_dev
    band = tiles // far_count
    first = lax.axis_index("clus") * tile_dev
    entry = lax.broadcasted_iota(jnp.int32, (far_count, tile_dev), 0)
    place = admissible_ref[...] - first - entry * band
    place = jnp.where(place < 0, place + tiles, place)
    place = jnp.where(place < 0, place + tiles, place)
    place = jnp.concatenate([place, place], axis=1)
    owner, tile = place // tile_dev, place % tile_dev
    lane = lax.broadcasted_iota(jnp.int32, (far_count, 2 * tile_dev), 1)
    part = jnp.where(lane < tile_dev, 0, GROUP)
    line = owner * 2 * tile_dev + (tile >> 3) * 2 * GROUP + part + (tile & (GROUP - 1))
    for k in range(far_count):
        hot_ref[k] = one_hot(hot_ref.shape[1], line[k : k + 1])


def pack_coupling(coupling_ref, packed_ref):
    half = packed_ref.shape[1]

    @pl.loop(0, packed_ref.shape[0])
    def _(r):
        for k in range(half):
            pair = [coupling_ref[k, r], coupling_ref[k + half, r]]
            packed_ref[r, k] = jnp.concatenate(pair, axis=1).astype(jnp.float32)


def far_mix(peers, coeff_ref, hot_ref, packed_ref, picked_ref, partial_ref, mixed_ref):
    rank, half = packed_ref.shape[:2]
    far_count, span, count = hot_ref.shape
    span //= count
    stride = peers // far_count
    tile_dev = count // 2

    def found(k):
        held = jnp.concatenate(
            [coeff_ref[(k * stride + j) % peers] for j in range(span)], axis=1
        )
        return jnp.dot(held, hot_ref[k], preferred_element_type=jnp.float32)

    for k in range(half):
        both = [found(k), found(k + half)]
        for c in range(2):
            own = slice(c * tile_dev, (c + 1) * tile_dev)
            picked_ref[c, k] = jnp.concatenate([one[:, own] for one in both], axis=1)

    @pl.loop(0, rank // MIX_STEP)
    def _(step):
        total = [[0.0, 0.0] for _ in range(MIX_STEP)]
        for k in range(half):
            held = [picked_ref[c, k] for c in range(2)]
            for j in range(MIX_STEP):
                block = packed_ref[step * MIX_STEP + j, k]
                total[j] = [total[j][c] + block * held[c] for c in range(2)]
        for c in range(2):
            for j in range(MIX_STEP):
                blocks = blocks_of(total[j][c])
                partial_ref[c, step * MIX_STEP + j] = functools.reduce(jnp.add, blocks)

    for c in range(2):
        for start in range(0, rank, GROUP):
            mixed_ref[c, start : start + GROUP, :] = fold_rows(
                [partial_ref[c, start + j] for j in range(GROUP)]
            )


def voltages(mixed_ref, basis_ref, near_ref, flow_ref, resistance_ref, voltage_ref):
    rank, tile_dev = mixed_ref.shape[1], mixed_ref.shape[2] // 2
    width = GROUP * rank
    repeat = lax.broadcasted_iota(jnp.int32, (rank, width), 1) % rank
    repeat = jnp.where(
        lax.broadcasted_iota(jnp.int32, (rank, width), 0) == repeat, 1.0, 0.0
    ).astype(jnp.bfloat16)
    both = mixed_ref[...]
    both = both[:, :, :tile_dev] + both[:, :, tile_dev:]
    turned = jnp.concatenate([both[0], both[1]], axis=1).T.astype(jnp.bfloat16)
    wide = jnp.dot(turned, repeat, preferred_element_type=jnp.float32)
    wide = [wide[:tile_dev], wide[tile_dev:]]
    mask = lax.broadcasted_iota(jnp.int32, (GROUP, width), 1) // rank
    mask = mask == lax.broadcasted_iota(jnp.int32, (GROUP, width), 0)
    for group in range(tile_dev // GROUP):
        own = slice(group * GROUP, (group + 1) * GROUP)
        mixed = jnp.concatenate([jnp.where(mask, wide[c][own], 0.0) for c in range(2)], axis=0)
        far = jnp.dot(
            mixed.astype(jnp.bfloat16),
            basis_ref[group * width : (group + 1) * width, :],
            preferred_element_type=jnp.float32,
        )
        place = slice(group * 2 * GROUP, (group + 1) * 2 * GROUP)
        reactive = near_ref[place, :] + far
        flow = flow_ref[place, :]
        resistance = resistance_ref[own, :]
        voltage = jnp.concatenate(
            [
                resistance * flow[:GROUP] - reactive[GROUP:],
                resistance * flow[GROUP:] + reactive[:GROUP],
            ],
            axis=0,
        )
        for part, value in enumerate(halves(voltage)):
            voltage_ref[part, place, :] = value


def port_sums(current, z_ref):
    products = [
        lax.dot_general(
            current,
            z_ref[part],
            NT,
            precision=lax.Precision.HIGHEST,
            preferred_element_type=jnp.float32,
        )
        for part in range(2)
    ]
    return [products[0][0:1] - products[1][1:2], products[0][1:2] + products[1][0:1]]


def whole_kernel(
    peers,
    need_hbm,
    current_hbm,
    port_hbm,
    entry_hbm,
    sign_hbm,
    basis_in_hbm,
    source_hbm,
    blocks_hbm,
    admissible_hbm,
    coupling_hbm,
    basis_out_hbm,
    resistance_hbm,
    z_hbm,
    o_ref,
    need_ref,
    current_ref,
    port_ref,
    entry_ref,
    sign_ref,
    basis_in_ref,
    source_ref,
    blocks_ref,
    admissible_ref,
    coupling_ref,
    basis_out_ref,
    resistance_ref,
    z_ref,
    asked_ref,
    reply_ref,
    answer_ref,
    flow_ref,
    coeff_ref,
    near_hot_ref,
    near_picked_ref,
    near_ref,
    far_hot_ref,
    packed_ref,
    sum_hot_ref,
    picked_ref,
    partial_ref,
    mixed_ref,
    voltage_ref,
    slots_ref,
    arrived_ref,
    send_sem,
    recv_sem,
    load_sem,
):
    me = lax.axis_index("clus")
    met = greet(peers)
    pairs = [
        (need_hbm, need_ref),
        (current_hbm, current_ref),
        (entry_hbm, entry_ref),
        (sign_hbm, sign_ref),
        (port_hbm, port_ref),
        (source_hbm, source_ref),
        (admissible_hbm, admissible_ref),
        (basis_in_hbm, basis_in_ref),
        (blocks_hbm, blocks_ref),
        (coupling_hbm, coupling_ref),
        (basis_out_hbm, basis_out_ref),
        (resistance_hbm, resistance_ref),
        (z_hbm, z_ref),
    ]
    loads = [
        pltpu.make_async_copy(source, target, load_sem.at[i])
        for i, (source, target) in enumerate(pairs)
    ]
    for load in loads:
        load.start()
    (
        need_load,
        current_load,
        entry_load,
        sign_load,
        port_load,
        source_load,
        admissible_load,
        basis_in_load,
        blocks_load,
        coupling_load,
        basis_out_load,
        resistance_load,
        z_load,
    ) = loads
    sems = (send_sem, recv_sem)
    mesh_rows = current_ref.shape[0]
    ports = port_ref.shape[1]
    asked_ref[me] = jnp.full(asked_ref.shape[1:], -1, jnp.int32)
    need_load.wait()
    met()
    half = peers // 2
    near_steps, far_steps = range(1, half), range(half, peers)
    near_first = lax.div(me, half) * half
    far_first = half - near_first
    needs = [
        push(
            peers,
            0,
            steps,
            lambda peer: need_ref.at[peer],
            lambda peer, own: asked_ref.at[own],
            *sems,
        )
        for steps in (far_steps, near_steps)
    ]
    current_load.wait()
    entry_load.wait()
    sign_load.wait()
    own_tables = [blocks_of(current_ref[:, c, :]) for c in range(2)]
    branch_flows(own_tables, 0, False, LOCAL_CHUNK, entry_ref, sign_ref, flow_ref)
    port_load.wait()
    port = jnp.concatenate(
        [port_ref[...], jnp.full((1, LANES - ports), -1, jnp.int32)], axis=1
    ) - me * (mesh_rows * LANES)
    port_row = port >> 7
    held = pick(own_tables, port & (LANES - 1), port_row)
    port_current = [fold(held[c]) for c in range(2)]
    replies = []
    for first, steps, (arrive, _) in (
        (far_first, far_steps, needs[0]),
        (near_first, near_steps, needs[1]),
    ):
        arrive()
        for start in range(0, half, GROUP // 2):
            found = []
            for j in range(GROUP // 2):
                asked = asked_ref[first + start + j]
                found += pick(own_tables, asked & (LANES - 1), asked >> 7)
            found = fold_rows(found)
            for j in range(GROUP // 2):
                reply_ref[first + start + j] = jnp.concatenate(
                    [found[2 * j : 2 * j + 2]] + port_current, axis=0
                )
        replies.append(
            push(
                peers,
                1,
                steps,
                lambda peer: reply_ref.at[peer],
                lambda peer, own: answer_ref.at[own],
                *sems,
            )
        )
    answer_ref[me] = jnp.concatenate([jnp.zeros((2, LANES), jnp.float32)] + port_current, axis=0)
    source_load.wait()
    near_choice(source_ref, near_hot_ref)
    admissible_load.wait()
    far_choice(peers, admissible_ref, far_hot_ref)
    coupling_load.wait()
    pack_coupling(coupling_ref, packed_ref)
    basis_in_load.wait()
    for first, (arrive, _) in zip((near_first, far_first), reversed(replies)):
        arrive()
        own = pl.ds(first, half)
        tables = [blocks_of(answer_ref[own, c, :]) for c in range(2)]
        branch_flows(
            tables, mesh_rows + first, True, REMOTE_CHUNK, entry_ref, sign_ref, flow_ref
        )
    far_coefficients(basis_in_ref, flow_ref, coeff_ref.at[0])
    arrive, leave_coeff = push(
        peers,
        2,
        range(1, peers),
        lambda peer: coeff_ref.at[0],
        lambda peer, own: coeff_ref.at[lax.rem(own - peer + peers, peers)],
        *sems,
    )
    blocks_load.wait()
    near_work(flow_ref, near_hot_ref, blocks_ref, near_picked_ref, near_ref)
    signed_hot(entry_ref, sign_ref, sum_hot_ref)
    basis_out_load.wait()
    resistance_load.wait()
    arrive()
    far_mix(peers, coeff_ref, far_hot_ref, packed_ref, picked_ref, partial_ref, mixed_ref)
    voltages(mixed_ref, basis_out_ref, near_ref, flow_ref, resistance_ref, voltage_ref)
    remote = collect(entry_ref, sum_hot_ref, voltage_ref, mesh_rows, peers, REMOTE_CHUNK)
    for c in range(2):
        slots_ref[:, c, :] = remote[c * peers : (c + 1) * peers, :]
    arrive, leave_slots = push(
        peers,
        3,
        range(1, peers),
        lambda peer: slots_ref.at[peer],
        lambda peer, own: arrived_ref.at[own],
        *sems,
    )
    arrived_ref[me] = jnp.zeros(arrived_ref.shape[1:], jnp.float32)
    local = collect(entry_ref, sum_hot_ref, voltage_ref, 0, mesh_rows, LOCAL_CHUNK)
    z_load.wait()
    current = answer_ref[0]
    for p in range(1, peers):
        current = current + answer_ref[p]
    port_voltage = [
        jnp.concatenate([value, jnp.zeros((1, LANES - ports), jnp.float32)], axis=1)
        for value in port_sums(current[2:4, :ports], z_ref)
    ]
    asked = jnp.concatenate([asked_ref[p] for p in range(peers)] + [port], axis=1)
    asked_hot = one_hot(LANES, asked & (LANES - 1))
    for _, leave in needs + replies:
        leave()
    leave_coeff()
    arrive()
    values = [
        jnp.concatenate([arrived_ref[p, c : c + 1] for p in range(peers)] + [port_voltage[c]], axis=1)
        for c in range(2)
    ]
    high, low = zip(*[halves(value) for value in values])
    spread = spread_over(high + low, asked >> 7, mesh_rows)
    made = add_up(spread, asked_hot)
    total = local + made[: 2 * mesh_rows] + made[2 * mesh_rows :]
    for c in range(2):
        o_ref[c] = total[c * mesh_rows : (c + 1) * mesh_rows]
    leave_slots()


def per_device(
    mesh_current,
    branch_entry,
    branch_sign,
    need_slots,
    resistance,
    near_blocks,
    near_source,
    basis_in,
    coupling,
    basis_out,
    admissible,
    port_mesh,
    port_coupling,
):
    peers = lax.axis_size("clus")
    mesh_dev = mesh_current.shape[1]
    tile_dev, near_count, tile_width = near_blocks.shape[:3]
    rank = basis_in.shape[1]
    mesh_rows = mesh_dev // LANES
    far_count = admissible.shape[1]
    band = peers * tile_dev // far_count
    span = (band + tile_dev - 2) // tile_dev + 1
    operands = [
        need_slots[:, None, :],
        mesh_current.reshape(2, mesh_rows, LANES).transpose(1, 0, 2),
        port_mesh[None, :],
        branch_entry,
        branch_sign,
        basis_in.reshape(tile_dev * rank, tile_width),
        near_source.T,
        near_blocks,
        admissible.T,
        coupling.transpose(1, 2, 3, 0),
        basis_out.reshape(tile_dev * rank, tile_width),
        resistance.reshape(tile_dev, tile_width),
        port_coupling,
    ]
    f32, bf16 = jnp.float32, jnp.bfloat16
    operands = [pltpu.with_memory_space_constraint(x, pltpu.HBM) for x in operands]
    tiles = pltpu.VMEM((2 * tile_dev, LANES), f32)
    message = pltpu.VMEM((peers, 2, LANES), f32)
    made = pl.pallas_call(
        functools.partial(whole_kernel, peers),
        out_shape=jax.ShapeDtypeStruct((2, mesh_rows, LANES), f32),
        in_specs=[pl.BlockSpec(memory_space=pltpu.HBM)] * len(operands),
        out_specs=pl.BlockSpec(memory_space=pltpu.VMEM),
        scratch_shapes=[pltpu.VMEM(x.shape, x.dtype) for x in operands]
        + [
            pltpu.VMEM((peers, 1, LANES), jnp.int32),
            pltpu.VMEM((peers, 4, LANES), f32),
            pltpu.VMEM((peers, 4, LANES), f32),
            tiles,
            pltpu.VMEM((peers, rank, 2 * tile_dev), bf16),
            pltpu.VMEM((near_count, 2 * tile_dev, 2 * tile_dev), bf16),
            pltpu.VMEM((2 * tile_dev, near_count * LANES), bf16),
            tiles,
            pltpu.VMEM((far_count, span * 2 * tile_dev, 2 * tile_dev), bf16),
            pltpu.VMEM((rank, far_count // 2, rank, 2 * tile_dev), f32),
            pltpu.VMEM((branch_entry.shape[0], LANES, branch_entry.shape[1]), bf16),
            pltpu.VMEM((2, far_count // 2, rank, 2 * tile_dev), f32),
            pltpu.VMEM((2, rank, GROUP, 2 * tile_dev), f32),
            pltpu.VMEM((2, rank, 2 * tile_dev), f32),
            pltpu.VMEM((2, 2 * tile_dev, LANES), f32),
            message,
            message,
            pltpu.SemaphoreType.DMA((4, peers)),
            pltpu.SemaphoreType.DMA((4, peers)),
            pltpu.SemaphoreType.DMA((len(operands),)),
        ],
        compiler_params=pltpu.CompilerParams(
            collective_id=0, has_side_effects=True, vmem_limit_bytes=VMEM_LIMIT
        ),
    )(*operands)
    return made.reshape(2, mesh_dev)


def solution(mesh):
    both = ("groups", "clus")
    in_specs = (
        P(None, both),
        P(None, both),
        P(None, both),
        P(both, None),
        P(both),
        P(both, None, None, None),
        P(both, None),
        P(both, None, None),
        P(both, None, None, None),
        P(both, None, None),
        P(both, None),
        P("groups"),
        P(),
    )
    return jax.shard_map(
        per_device, mesh=mesh, in_specs=in_specs, out_specs=P(None, both), check_vma=False
    )
```

```python
import functools

import jax
import jax.numpy as jnp
from jax import lax
from jax.experimental import pallas as pl
from jax.experimental.pallas import tpu as pltpu
from jax.sharding import PartitionSpec as P

LANES = 128
GROUP = 8
LOCAL_CHUNK = 2048
REMOTE_CHUNK = 8192
HOT_CHUNK = 1024
MIX_STEP = 8
VMEM_LIMIT = 44 * 1024 * 1024
NT = (((1,), (1,)), ((), ()))


def partner(peers, step):
    me = lax.axis_index("clus")
    peer, bit = me, 1
    while bit < peers:
        if step & bit:
            peer = peer + bit * (1 - 2 * lax.rem(lax.div(me, bit), 2))
        bit *= 2
    return peer


def greet(peers):
    barrier = pltpu.get_barrier_semaphore()
    for step in reversed(range(1, peers)):
        pl.semaphore_signal(
            barrier,
            inc=1,
            device_id={"clus": partner(peers, step)},
            device_id_type=pl.DeviceIdType.MESH,
        )
    return lambda: pl.semaphore_wait(barrier, peers - 1)


def push(peers, phase, steps, source_at, target_at, send_sem, recv_sem):
    me = lax.axis_index("clus")
    copies = []
    for step in reversed(steps):
        peer = partner(peers, step)
        copy = pltpu.make_async_remote_copy(
            src_ref=source_at(peer),
            dst_ref=target_at(peer, me),
            send_sem=send_sem.at[phase, step],
            recv_sem=recv_sem.at[phase, step],
            device_id={"clus": peer},
            device_id_type=pl.DeviceIdType.MESH,
        )
        copy.start()
        copies.append(copy)

    def arrive():
        for copy in copies:
            copy.wait_recv()

    def leave():
        for copy in copies:
            copy.wait_send()

    return arrive, leave


def one_hot(rows, index):
    match = lax.broadcasted_iota(jnp.int32, (rows, index.shape[1]), 0) == index
    return jnp.where(match, 1.0, 0.0).astype(jnp.bfloat16)


def pick(tables, low, row):
    sub = lax.broadcasted_iota(jnp.int32, (GROUP, LANES), 0)
    lanes = jnp.broadcast_to(low, (GROUP, LANES))
    gap = jnp.broadcast_to(row, (GROUP, LANES)) - sub
    total = [0.0, 0.0]
    for block in range(len(tables[0])):
        match = gap == block * GROUP
        for c in range(2):
            found = jnp.take_along_axis(
                tables[c][block], lanes, axis=1, mode="promise_in_bounds"
            )
            total[c] += jnp.where(match, found, 0.0)
    return total


def fold(value):
    return jnp.sum(value, axis=0, keepdims=True)


def fold_rows(values):
    line = lax.broadcasted_iota(jnp.int32, (GROUP, LANES), 0)
    gap = GROUP // 2
    while gap:
        low = (line & gap) == 0

        def swap(value):
            down = pltpu.roll(value, gap, 0)
            if 2 * gap == GROUP:
                return down
            return jnp.where(low, pltpu.roll(value, GROUP - gap, 0), down)

        half = len(values) // 2
        values = [
            jnp.where(low, one, two) + swap(jnp.where(low, two, one))
            for one, two in zip(values[:half], values[half:])
        ]
        gap //= 2
    return values[0]


def blocks_of(table):
    return [table[start : start + GROUP] for start in range(0, table.shape[0], GROUP)]


def branch_flows(tables, first_row, add, chunk, entry_ref, sign_ref, flow_ref):
    chunk = min(chunk, entry_ref.shape[1])
    groups = chunk // (GROUP * LANES)

    @pl.loop(0, entry_ref.shape[1] // chunk)
    def _(step):
        for group in range(groups):
            rows = [[], []]
            for j in range(GROUP):
                start = step * chunk + (group * GROUP + j) * LANES
                columns = pl.ds(pl.multiple_of(start, LANES), LANES)
                total = [0.0, 0.0]
                for k in range(entry_ref.shape[0]):
                    entry = entry_ref[k : k + 1, columns]
                    orient = (2 * sign_ref[k : k + 1, columns] - 1).astype(jnp.float32)
                    found = pick(tables, entry & (LANES - 1), (entry >> 7) - first_row)
                    total = [total[c] + orient * found[c] for c in range(2)]
                for c in range(2):
                    rows[c].append(total[c])
            for c in range(2):
                start = (step * groups + group) * 2 * GROUP + c * GROUP
                place = pl.ds(pl.multiple_of(start, GROUP), GROUP)
                made = fold_rows(rows[c])
                flow_ref[place, :] = flow_ref[place, :] + made if add else made


def signed_hot(entry_ref, sign_ref, hot_ref):
    @pl.loop(0, entry_ref.shape[1] // HOT_CHUNK)
    def _(step):
        columns = pl.ds(pl.multiple_of(step * HOT_CHUNK, HOT_CHUNK), HOT_CHUNK)
        for k in range(entry_ref.shape[0]):
            orient = (2 * sign_ref[k : k + 1, columns] - 1).astype(jnp.float32)
            low = entry_ref[k : k + 1, columns] & (LANES - 1)
            match = lax.broadcasted_iota(jnp.int32, (LANES, HOT_CHUNK), 0) == low
            hot_ref[k, :, columns] = jnp.where(match, orient, 0.0).astype(jnp.bfloat16)


def halves(value):
    high = value.astype(jnp.bfloat16).astype(jnp.float32)
    return high, value - high


def spread_over(parts, row, rows):
    mask = lax.broadcasted_iota(jnp.int32, (rows, row.shape[1]), 0) == row
    return jnp.concatenate(
        [jnp.where(mask, part, 0.0).astype(jnp.bfloat16) for part in parts], axis=0
    )


def add_up(hot, spread):
    return lax.dot_general(hot, spread, NT, preferred_element_type=jnp.float32)


def join(made):
    turned = made.T
    half = turned.shape[0] // 2
    return turned[:half] + turned[half:]


def collect(entry_ref, hot_ref, voltage_ref, first_row, rows, chunk):
    count = entry_ref.shape[1]
    chunk = min(chunk, count)
    groups = chunk // (GROUP * LANES)

    def body(step, total):
        columns = pl.ds(pl.multiple_of(step * chunk, chunk), chunk)
        parts = []
        for part in range(2):
            for c in range(2):
                lines = []
                for group in range(groups):
                    start = (step * groups + group) * 2 * GROUP + c * GROUP
                    tile = voltage_ref[part, pl.ds(pl.multiple_of(start, GROUP), GROUP), :]
                    lines += [tile[j : j + 1] for j in range(GROUP)]
                parts.append(jnp.concatenate(lines, axis=1))
        for k in range(entry_ref.shape[0]):
            row = (entry_ref[k : k + 1, columns] >> 7) - first_row
            total += add_up(hot_ref[k, :, columns], spread_over(parts, row, rows))
        return total

    total = jnp.zeros((LANES, 4 * rows), jnp.float32)
    if count == chunk:
        return join(body(0, total))
    return join(lax.fori_loop(0, count // chunk, body, total))


def far_coefficients(basis_ref, flow_ref, o_ref):
    flows = flow_ref[...].astype(jnp.bfloat16)
    count = flows.shape[0]
    tile_dev = count // 2
    rank = basis_ref.shape[0] // tile_dev
    lane = lax.broadcasted_iota(jnp.int32, (rank, count), 1)
    tile = (lane >> 4) * GROUP + (lane & (GROUP - 1))
    total = jnp.zeros((rank, count), jnp.float32)
    for start in range(0, tile_dev, GROUP):
        crossed = lax.dot_general(
            basis_ref[start * rank : (start + GROUP) * rank, :],
            flows,
            NT,
            preferred_element_type=jnp.float32,
        )
        for j in range(GROUP):
            total = jnp.where(tile == start + j, crossed[j * rank : (j + 1) * rank], total)
    o_ref[...] = total.astype(jnp.bfloat16)


def near_choice(source_ref, hot_ref):
    near_count, tile_dev = source_ref.shape
    count = 2 * tile_dev
    lane = lax.broadcasted_iota(jnp.int32, (tile_dev, count), 1)
    tile = (lane >> 4) * GROUP + (lane & (GROUP - 1))
    widen = lax.broadcasted_iota(jnp.int32, (tile_dev, count), 0) == tile
    source = jnp.dot(
        source_ref[...].astype(jnp.float32).astype(jnp.bfloat16),
        jnp.where(widen, 1.0, 0.0).astype(jnp.bfloat16),
        preferred_element_type=jnp.float32,
    ).astype(jnp.int32)
    part = lax.broadcasted_iota(jnp.int32, (near_count, count), 1) & GROUP
    place = (source >> 3) * 2 * GROUP + part + (source & (GROUP - 1))
    for k in range(near_count):
        hot = jnp.where(
            lax.broadcasted_iota(jnp.int32, (count, count), 0) == place[k : k + 1], 1.0, 0.0
        )
        hot_ref[k] = hot.T.astype(jnp.bfloat16)


def near_work(flow_ref, hot_ref, blocks_ref, picked_ref, near_ref):
    near_count = blocks_ref.shape[1]
    flows = flow_ref[...].astype(jnp.bfloat16)
    for k in range(near_count):
        picked_ref[:, k * LANES : (k + 1) * LANES] = jnp.dot(
            hot_ref[k], flows, preferred_element_type=jnp.float32
        ).astype(jnp.bfloat16)

    @pl.loop(0, blocks_ref.shape[0] // GROUP)
    def _(step):
        place = pl.ds(pl.multiple_of(step * 2 * GROUP, 2 * GROUP), 2 * GROUP)
        source = picked_ref[place, :]
        row = lax.broadcasted_iota(jnp.int32, (2 * GROUP, LANES), 0) & (GROUP - 1)
        total = jnp.zeros((2 * GROUP, LANES), jnp.float32)
        for j in range(GROUP):
            block = jnp.concatenate(
                [blocks_ref[step * GROUP + j, k] for k in range(near_count)], axis=1
            )
            made = lax.dot_general(source, block, NT, preferred_element_type=jnp.float32)
            total = jnp.where(row == j, made, total)
        near_ref[place, :] = total


def far_choice(peers, admissible_ref, hot_ref):
    far_count, tile_dev = admissible_ref.shape
    tiles = peers * tile_dev
    band = tiles // far_count
    first = lax.axis_index("clus") * tile_dev
    entry = lax.broadcasted_iota(jnp.int32, (far_count, tile_dev), 0)
    place = admissible_ref[...] - first - entry * band
    place = jnp.where(place < 0, place + tiles, place)
    place = jnp.where(place < 0, place + tiles, place)
    place = jnp.concatenate([place, place], axis=1)
    owner, tile = place // tile_dev, place % tile_dev
    lane = lax.broadcasted_iota(jnp.int32, (far_count, 2 * tile_dev), 1)
    part = jnp.where(lane < tile_dev, 0, GROUP)
    line = owner * 2 * tile_dev + (tile >> 3) * 2 * GROUP + part + (tile & (GROUP - 1))
    for k in range(far_count):
        hot_ref[k] = one_hot(hot_ref.shape[1], line[k : k + 1])


def pack_coupling(coupling_ref, packed_ref):
    half = packed_ref.shape[1]

    @pl.loop(0, packed_ref.shape[0])
    def _(r):
        for k in range(half):
            pair = [coupling_ref[k, r], coupling_ref[k + half, r]]
            packed_ref[r, k] = jnp.concatenate(pair, axis=1).astype(jnp.float32)


def far_mix(peers, coeff_ref, hot_ref, packed_ref, picked_ref, partial_ref, mixed_ref):
    rank, half = packed_ref.shape[:2]
    far_count, span, count = hot_ref.shape
    span //= count
    stride = peers // far_count
    tile_dev = count // 2

    def found(k):
        held = jnp.concatenate(
            [coeff_ref[(k * stride + j) % peers] for j in range(span)], axis=1
        )
        return jnp.dot(held, hot_ref[k], preferred_element_type=jnp.float32)

    for k in range(half):
        both = [found(k), found(k + half)]
        for c in range(2):
            own = slice(c * tile_dev, (c + 1) * tile_dev)
            picked_ref[c, k] = jnp.concatenate([one[:, own] for one in both], axis=1)

    @pl.loop(0, rank // MIX_STEP)
    def _(step):
        total = [[0.0, 0.0] for _ in range(MIX_STEP)]
        for k in range(half):
            held = [picked_ref[c, k] for c in range(2)]
            for j in range(MIX_STEP):
                block = packed_ref[step * MIX_STEP + j, k]
                total[j] = [total[j][c] + block * held[c] for c in range(2)]
        for c in range(2):
            for j in range(MIX_STEP):
                blocks = blocks_of(total[j][c])
                partial_ref[c, step * MIX_STEP + j] = functools.reduce(jnp.add, blocks)

    for c in range(2):
        for start in range(0, rank, GROUP):
            mixed_ref[c, start : start + GROUP, :] = fold_rows(
                [partial_ref[c, start + j] for j in range(GROUP)]
            )


def base_voltages(near_ref, flow_ref, resistance_ref, base_ref):
    for group in range(resistance_ref.shape[0] // GROUP):
        place = slice(group * 2 * GROUP, (group + 1) * 2 * GROUP)
        resistance = resistance_ref[group * GROUP : (group + 1) * GROUP, :]
        reactive, flow = near_ref[place, :], flow_ref[place, :]
        base_ref[place, :] = jnp.concatenate(
            [
                resistance * flow[:GROUP] - reactive[GROUP:],
                resistance * flow[GROUP:] + reactive[:GROUP],
            ],
            axis=0,
        )


def voltages(mixed_ref, basis_ref, base_ref, voltage_ref):
    rank, tile_dev = mixed_ref.shape[1], mixed_ref.shape[2] // 2
    width = GROUP * rank
    repeat = lax.broadcasted_iota(jnp.int32, (rank, width), 1) % rank
    repeat = jnp.where(
        lax.broadcasted_iota(jnp.int32, (rank, width), 0) == repeat, 1.0, 0.0
    ).astype(jnp.bfloat16)
    both = mixed_ref[...]
    both = both[:, :, :tile_dev] + both[:, :, tile_dev:]
    turned = jnp.concatenate([both[0], both[1]], axis=1).T.astype(jnp.bfloat16)
    wide = jnp.dot(turned, repeat, preferred_element_type=jnp.float32)
    wide = [wide[:tile_dev], wide[tile_dev:]]
    mask = lax.broadcasted_iota(jnp.int32, (GROUP, width), 1) // rank
    mask = mask == lax.broadcasted_iota(jnp.int32, (GROUP, width), 0)
    for group in range(tile_dev // GROUP):
        own = slice(group * GROUP, (group + 1) * GROUP)
        mixed = jnp.concatenate([jnp.where(mask, wide[c][own], 0.0) for c in range(2)], axis=0)
        far = jnp.dot(
            mixed.astype(jnp.bfloat16),
            basis_ref[group * width : (group + 1) * width, :],
            preferred_element_type=jnp.float32,
        )
        place = slice(group * 2 * GROUP, (group + 1) * 2 * GROUP)
        base = base_ref[place, :]
        voltage = jnp.concatenate(
            [base[:GROUP] - far[GROUP:], base[GROUP:] + far[:GROUP]], axis=0
        )
        for part, value in enumerate(halves(voltage)):
            voltage_ref[part, place, :] = value


def port_sums(current, z_ref):
    products = [
        lax.dot_general(
            current,
            z_ref[part],
            NT,
            precision=lax.Precision.HIGHEST,
            preferred_element_type=jnp.float32,
        )
        for part in range(2)
    ]
    return [products[0][0:1] - products[1][1:2], products[0][1:2] + products[1][0:1]]


def whole_kernel(
    peers,
    need_hbm,
    current_hbm,
    port_hbm,
    entry_hbm,
    sign_hbm,
    basis_in_hbm,
    source_hbm,
    blocks_hbm,
    admissible_hbm,
    coupling_hbm,
    basis_out_hbm,
    resistance_hbm,
    z_hbm,
    o_ref,
    need_ref,
    current_ref,
    port_ref,
    entry_ref,
    sign_ref,
    basis_in_ref,
    source_ref,
    blocks_ref,
    admissible_ref,
    coupling_ref,
    basis_out_ref,
    resistance_ref,
    z_ref,
    asked_ref,
    reply_ref,
    answer_ref,
    flow_ref,
    coeff_ref,
    near_hot_ref,
    near_picked_ref,
    near_ref,
    far_hot_ref,
    packed_ref,
    sum_hot_ref,
    picked_ref,
    partial_ref,
    mixed_ref,
    base_ref,
    voltage_ref,
    slots_ref,
    arrived_ref,
    send_sem,
    recv_sem,
    load_sem,
):
    me = lax.axis_index("clus")
    met = greet(peers)
    pairs = [
        (need_hbm, need_ref),
        (current_hbm, current_ref),
        (entry_hbm, entry_ref),
        (sign_hbm, sign_ref),
        (port_hbm, port_ref),
        (source_hbm, source_ref),
        (admissible_hbm, admissible_ref),
        (basis_in_hbm, basis_in_ref),
        (blocks_hbm, blocks_ref),
        (coupling_hbm, coupling_ref),
        (basis_out_hbm, basis_out_ref),
        (resistance_hbm, resistance_ref),
        (z_hbm, z_ref),
    ]
    loads = [
        pltpu.make_async_copy(source, target, load_sem.at[i])
        for i, (source, target) in enumerate(pairs)
    ]
    for load in loads:
        load.start()
    (
        need_load,
        current_load,
        entry_load,
        sign_load,
        port_load,
        source_load,
        admissible_load,
        basis_in_load,
        blocks_load,
        coupling_load,
        basis_out_load,
        resistance_load,
        z_load,
    ) = loads
    sems = (send_sem, recv_sem)
    mesh_rows = current_ref.shape[0]
    ports = port_ref.shape[1]
    asked_ref[me] = jnp.full(asked_ref.shape[1:], -1, jnp.int32)
    need_load.wait()
    met()
    half = peers // 2
    near_steps, far_steps = range(1, half), range(half, peers)
    near_first = lax.div(me, half) * half
    far_first = half - near_first
    needs = [
        push(
            peers,
            0,
            steps,
            lambda peer: need_ref.at[peer],
            lambda peer, own: asked_ref.at[own],
            *sems,
        )
        for steps in (far_steps, near_steps)
    ]
    current_load.wait()
    entry_load.wait()
    sign_load.wait()
    own_tables = [blocks_of(current_ref[:, c, :]) for c in range(2)]
    branch_flows(own_tables, 0, False, LOCAL_CHUNK, entry_ref, sign_ref, flow_ref)
    port_load.wait()
    port = jnp.concatenate(
        [port_ref[...], jnp.full((1, LANES - ports), -1, jnp.int32)], axis=1
    ) - me * (mesh_rows * LANES)
    port_row = port >> 7
    held = pick(own_tables, port & (LANES - 1), port_row)
    port_current = [fold(held[c]) for c in range(2)]
    replies = []
    for first, steps, (arrive, _) in (
        (far_first, far_steps, needs[0]),
        (near_first, near_steps, needs[1]),
    ):
        arrive()
        for start in range(0, half, GROUP // 2):
            found = []
            for j in range(GROUP // 2):
                asked = asked_ref[first + start + j]
                found += pick(own_tables, asked & (LANES - 1), asked >> 7)
            found = fold_rows(found)
            for j in range(GROUP // 2):
                reply_ref[first + start + j] = jnp.concatenate(
                    [found[2 * j : 2 * j + 2]] + port_current, axis=0
                )
        replies.append(
            push(
                peers,
                1,
                steps,
                lambda peer: reply_ref.at[peer],
                lambda peer, own: answer_ref.at[own],
                *sems,
            )
        )
    answer_ref[me] = jnp.concatenate([jnp.zeros((2, LANES), jnp.float32)] + port_current, axis=0)
    source_load.wait()
    near_choice(source_ref, near_hot_ref)
    admissible_load.wait()
    far_choice(peers, admissible_ref, far_hot_ref)
    coupling_load.wait()
    pack_coupling(coupling_ref, packed_ref)
    basis_in_load.wait()
    for first, (arrive, _) in zip((near_first, far_first), reversed(replies)):
        arrive()
        own = pl.ds(first, half)
        tables = [blocks_of(answer_ref[own, c, :]) for c in range(2)]
        branch_flows(
            tables, mesh_rows + first, True, REMOTE_CHUNK, entry_ref, sign_ref, flow_ref
        )
    far_coefficients(basis_in_ref, flow_ref, coeff_ref.at[0])
    arrive, leave_coeff = push(
        peers,
        2,
        range(1, peers),
        lambda peer: coeff_ref.at[0],
        lambda peer, own: coeff_ref.at[lax.rem(own - peer + peers, peers)],
        *sems,
    )
    blocks_load.wait()
    near_work(flow_ref, near_hot_ref, blocks_ref, near_picked_ref, near_ref)
    signed_hot(entry_ref, sign_ref, sum_hot_ref)
    basis_out_load.wait()
    resistance_load.wait()
    base_voltages(near_ref, flow_ref, resistance_ref, base_ref)
    arrive()
    far_mix(peers, coeff_ref, far_hot_ref, packed_ref, picked_ref, partial_ref, mixed_ref)
    voltages(mixed_ref, basis_out_ref, base_ref, voltage_ref)
    remote = collect(entry_ref, sum_hot_ref, voltage_ref, mesh_rows, peers, REMOTE_CHUNK)
    for c in range(2):
        slots_ref[:, c, :] = remote[c * peers : (c + 1) * peers, :]
    slots = [
        push(
            peers,
            3,
            steps,
            lambda peer: slots_ref.at[peer],
            lambda peer, own: arrived_ref.at[own],
            *sems,
        )
        for steps in (far_steps, near_steps)
    ]
    arrived_ref[me] = jnp.zeros(arrived_ref.shape[1:], jnp.float32)
    local = collect(entry_ref, sum_hot_ref, voltage_ref, 0, mesh_rows, LOCAL_CHUNK)
    z_load.wait()
    current = answer_ref[0]
    for p in range(1, peers):
        current = current + answer_ref[p]
    port_voltage = [
        jnp.concatenate([value, jnp.zeros((1, LANES - ports), jnp.float32)], axis=1)
        for value in port_sums(current[2:4, :ports], z_ref)
    ]
    for _, leave in needs + replies:
        leave()
    leave_coeff()
    total, extra, place = local, port_voltage, port
    for first, (arrive, _) in zip((near_first, far_first), reversed(slots)):
        index = [asked_ref[first + j] for j in range(half)]
        index = jnp.concatenate(index + ([] if extra is None else [place]), axis=1)
        asked_hot = one_hot(LANES, index & (LANES - 1))
        arrive()
        values = []
        for c in range(2):
            line = [arrived_ref[first + j, c : c + 1] for j in range(half)]
            line += [] if extra is None else [extra[c]]
            values.append(jnp.concatenate(line, axis=1))
        high, low = zip(*[halves(value) for value in values])
        made = add_up(spread_over(high + low, index >> 7, mesh_rows), asked_hot)
        total = total + made[: 2 * mesh_rows] + made[2 * mesh_rows :]
        extra = None
    for c in range(2):
        o_ref[c] = total[c * mesh_rows : (c + 1) * mesh_rows]
    for _, leave in slots:
        leave()


def per_device(
    mesh_current,
    branch_entry,
    branch_sign,
    need_slots,
    resistance,
    near_blocks,
    near_source,
    basis_in,
    coupling,
    basis_out,
    admissible,
    port_mesh,
    port_coupling,
):
    peers = lax.axis_size("clus")
    mesh_dev = mesh_current.shape[1]
    tile_dev, near_count, tile_width = near_blocks.shape[:3]
    rank = basis_in.shape[1]
    mesh_rows = mesh_dev // LANES
    far_count = admissible.shape[1]
    band = peers * tile_dev // far_count
    span = (band + tile_dev - 2) // tile_dev + 1
    operands = [
        need_slots[:, None, :],
        mesh_current.reshape(2, mesh_rows, LANES).transpose(1, 0, 2),
        port_mesh[None, :],
        branch_entry,
        branch_sign,
        basis_in.reshape(tile_dev * rank, tile_width),
        near_source.T,
        near_blocks,
        admissible.T,
        coupling.transpose(1, 2, 3, 0),
        basis_out.reshape(tile_dev * rank, tile_width),
        resistance.reshape(tile_dev, tile_width),
        port_coupling,
    ]
    f32, bf16 = jnp.float32, jnp.bfloat16
    operands = [pltpu.with_memory_space_constraint(x, pltpu.HBM) for x in operands]
    tiles = pltpu.VMEM((2 * tile_dev, LANES), f32)
    message = pltpu.VMEM((peers, 2, LANES), f32)
    made = pl.pallas_call(
        functools.partial(whole_kernel, peers),
        out_shape=jax.ShapeDtypeStruct((2, mesh_rows, LANES), f32),
        in_specs=[pl.BlockSpec(memory_space=pltpu.HBM)] * len(operands),
        out_specs=pl.BlockSpec(memory_space=pltpu.VMEM),
        scratch_shapes=[pltpu.VMEM(x.shape, x.dtype) for x in operands]
        + [
            pltpu.VMEM((peers, 1, LANES), jnp.int32),
            pltpu.VMEM((peers, 4, LANES), f32),
            pltpu.VMEM((peers, 4, LANES), f32),
            tiles,
            pltpu.VMEM((peers, rank, 2 * tile_dev), bf16),
            pltpu.VMEM((near_count, 2 * tile_dev, 2 * tile_dev), bf16),
            pltpu.VMEM((2 * tile_dev, near_count * LANES), bf16),
            tiles,
            pltpu.VMEM((far_count, span * 2 * tile_dev, 2 * tile_dev), bf16),
            pltpu.VMEM((rank, far_count // 2, rank, 2 * tile_dev), f32),
            pltpu.VMEM((branch_entry.shape[0], LANES, branch_entry.shape[1]), bf16),
            pltpu.VMEM((2, far_count // 2, rank, 2 * tile_dev), f32),
            pltpu.VMEM((2, rank, GROUP, 2 * tile_dev), f32),
            pltpu.VMEM((2, rank, 2 * tile_dev), f32),
            tiles,
            pltpu.VMEM((2, 2 * tile_dev, LANES), f32),
            message,
            message,
            pltpu.SemaphoreType.DMA((4, peers)),
            pltpu.SemaphoreType.DMA((4, peers)),
            pltpu.SemaphoreType.DMA((len(operands),)),
        ],
        compiler_params=pltpu.CompilerParams(
            collective_id=0, has_side_effects=True, vmem_limit_bytes=VMEM_LIMIT
        ),
    )(*operands)
    return made.reshape(2, mesh_dev)


def solution(mesh):
    both = ("groups", "clus")
    in_specs = (
        P(None, both),
        P(None, both),
        P(None, both),
        P(both, None),
        P(both),
        P(both, None, None, None),
        P(both, None),
        P(both, None, None),
        P(both, None, None, None),
        P(both, None, None),
        P(both, None),
        P("groups"),
        P(),
    )
    return jax.shard_map(
        per_device, mesh=mesh, in_specs=in_specs, out_specs=P(None, both), check_vma=False
    )
```
